32 devices in a mesh: seq: 4 (over z), fsdp: 2 (over y), dp: 4 (over x, core).
Axes of the slice: x: 2, y: 2, z: 4, core: 2. Of those that a mesh axis runs over, the one named last changes fastest.
Arguments:
- query: bfloat16 [8, 768, 1024], P(('fsdp', 'dp'), 'seq'), may hold values from -6 to 6
- key: bfloat16 [8, 768, 1024], P(('fsdp', 'dp'), 'seq'), may hold values from -6 to 6
- value: bfloat16 [8, 768, 1024], P(('fsdp', 'dp'), 'seq'), may hold values from -4 to 4
- out_weight: bfloat16 [1024, 2048], P('fsdp'), may hold values from -0.1875 to 0.1875
- out_grad: bfloat16 [8, 768, 2048], P(('fsdp', 'dp'), 'seq'), may hold values from -5 to 5
- block_ids: int32 [8], P('seq'), may hold values from 0 to 7, as said below
Outputs:
- query_grad: bfloat16 [8, 768, 1024], P(('fsdp', 'dp'), 'seq')
- key_grad: bfloat16 [8, 768, 1024], P(('fsdp', 'dp'), 'seq')
- value_grad: bfloat16 [8, 768, 1024], P(('fsdp', 'dp'), 'seq')
- weight_grad: bfloat16 [1024, 2048], P('fsdp')
The draws below stay inside these ranges and needn't reach their ends.
Inputs may be any that keep to these rules, and one draw needn't show every extreme that they name: `block_ids`: each number 0 to 7 appears once, and entries 2 i and 2 i + 1 always sum to 7.
All inputs are finite; a program needn't handle non-finite values.
Results may differ from the reference program's by a relative error of at most 0.027.
Values may be sent and summed in bfloat16 or wider, within the bound.
A program may use at most 64 MiB of HBM per device.

```python
import math
import jax
import jax.numpy as jnp
from jax import lax

D = 2048
HEADS = 8
HD = 128
BLOCK = 96
HQ = 1024
TOK_DEV = 192
BLOCKS = 8
LENGTH = 768
SEQS = 8


def float_rows(key, salt):
    noise_key = jax.random.fold_in(key, salt)
    base = jnp.clip(jax.random.normal(noise_key, (SEQS, LENGTH, HQ), jnp.float32), -4.0, 4.0)
    return base


def draw_query(key, part):
    base = float_rows(key, 11)
    return base.astype(jnp.bfloat16)


def draw_key(key, part):
    base = float_rows(key, 12)
    return base.astype(jnp.bfloat16)


def draw_block_ids(key, part):
    pairs = BLOCKS // 2
    order = jax.random.permutation(jax.random.fold_in(key, 7), pairs).astype(jnp.int32)
    flips = jax.random.randint(jax.random.fold_in(key, 8), (pairs,), 0, 2).astype(jnp.int32)
    first = jnp.where(flips == 1, BLOCKS - 1 - order, order)
    return jnp.stack([first, BLOCKS - 1 - first], axis=1).reshape(BLOCKS).astype(jnp.int32)


def block_scale(key, dims, shards, smallest, top_value):
    def one(dim, blocks):
        draws = jax.random.uniform(jax.random.fold_in(jax.random.fold_in(key, 6), dim), (blocks,), jnp.float32, smallest / len(shards), top_value / len(shards))
        return jnp.repeat(jnp.exp(draws), dims[dim] // blocks).reshape((-1,) + (1,) * (len(dims) - dim - 1))

    gain = one(*shards[0])
    for cut in shards[1:]:
        gain = gain * one(*cut)
    return gain


def bell_draw(stream_key, dims, width, reach, cuts=(), kind=jnp.bfloat16):
    drawn = jax.random.normal(stream_key, dims, jnp.float32) * width
    if len(cuts) > 0:
        drawn = block_scale(stream_key, dims, cuts, -0.22, 0.18) * drawn
    return jnp.clip(drawn, min=-reach, max=reach).astype(kind)


def setup_inputs(seed: int = 0) -> dict:
    arg_keys = jax.random.split(jax.random.key(seed), 7)
    query = draw_query(jax.random.fold_in(arg_keys[6], 71), 0)
    key = draw_key(jax.random.fold_in(arg_keys[6], 71), 0)
    value = bell_draw(arg_keys[2], (SEQS, LENGTH, HQ), 1.0, 4.0, ((0, 8), (1, 4)))
    out_weight = bell_draw(arg_keys[3], (HQ, D), HQ ** -0.5, 0.1875, ((0, 2),))
    out_grad = bell_draw(arg_keys[4], (SEQS, LENGTH, D), 1.0, 5.0, ((0, 8), (1, 4)))
    block_ids = draw_block_ids(jax.random.fold_in(arg_keys[6], 71), 0)
    return dict(query=query, key=key, value=value, out_weight=out_weight, out_grad=out_grad, block_ids=block_ids)


def lowered(values):
    return lax.optimization_barrier(values.astype(jnp.bfloat16)).astype(jnp.float32)

def sequence_terms(query_rows, key_rows, value_rows, grad_rows, out_weight, positions):
    score_scale = 1.0 / math.sqrt(HD)
    query_heads = query_rows.astype(jnp.float32).reshape(LENGTH, HEADS, HD)
    key_heads = key_rows.astype(jnp.float32).reshape(LENGTH, HEADS, HD)
    value_heads = value_rows.astype(jnp.float32).reshape(LENGTH, HEADS, HD)
    scores = jnp.einsum('qhd,khd->hqk', query_heads, key_heads) * score_scale
    allowed = positions[None, :] <= positions[:, None]
    scores = jnp.where(allowed[None], scores, -jnp.inf)
    row_top = lax.optimization_barrier(jnp.max(scores, axis=2, keepdims=True))
    row_total = lax.optimization_barrier(jnp.sum(jnp.exp(scores - row_top), axis=2, keepdims=True))
    log_total = row_top + jnp.log(row_total)
    probs = jnp.exp(scores - log_total)
    probs_low = lowered(probs)
    attended = lowered(jnp.einsum('hqk,khd->qhd', probs_low, value_heads))
    attn_grad = lowered(jnp.dot(grad_rows, out_weight.T, preferred_element_type=jnp.float32))
    grad_heads = attn_grad.reshape(LENGTH, HEADS, HD)
    attended_flat = attended.reshape(LENGTH, HQ)
    partials = jnp.einsum('btc,btd->bcd', attended_flat.reshape(-1, TOK_DEV, HQ), grad_rows.astype(jnp.float32).reshape(-1, TOK_DEV, D))
    weight_part = lax.optimization_barrier(jnp.sum(lowered(partials), axis=0))
    row_delta = jnp.einsum('qhd,qhd->hq', grad_heads, attended)
    prob_grad = jnp.einsum('qhd,khd->hqk', grad_heads, value_heads)
    score_grad = lowered(probs * (prob_grad - row_delta[:, :, None]))
    query_grad = (jnp.einsum('hqk,khd->qhd', score_grad, key_heads) * score_scale).astype(jnp.bfloat16)
    key_grad = (jnp.einsum('hqk,qhd->khd', score_grad, query_heads) * score_scale).astype(jnp.bfloat16)
    value_grad = jnp.einsum('hqk,qhd->khd', probs_low, grad_heads).astype(jnp.bfloat16)
    return (query_grad.reshape(LENGTH, HQ), key_grad.reshape(LENGTH, HQ), value_grad.reshape(LENGTH, HQ), weight_part)

def reference(query, key, value, out_weight, out_grad, block_ids):
    offsets = jnp.arange(BLOCK, dtype=jnp.int32)
    positions = (block_ids[:, None].astype(jnp.int32) * BLOCK + offsets[None, :]).reshape(LENGTH)

    def one_sequence(running, inputs):
        results = sequence_terms(inputs[0], inputs[1], inputs[2], inputs[3], out_weight, positions)
        return (running + results[3], (results[0], results[1], results[2]))
    start_sum = jnp.zeros((HQ, D), jnp.float32)
    grad_total, outputs = lax.scan(one_sequence, start_sum, (query, key, value, out_grad))
    weight_grad = (grad_total * (1.0 / math.sqrt(SEQS * LENGTH))).astype(jnp.bfloat16)
    return (outputs[0], outputs[1], outputs[2], weight_grad)
```

```python
import functools
import math

import jax
import jax.numpy as jnp
from jax import lax
from jax.experimental import pallas as pl
from jax.experimental.pallas import tpu as pltpu
from jax.sharding import PartitionSpec as P

HEADS = 8
HD = 128
MESH = pl.DeviceIdType.MESH
F32 = jnp.float32
BF16 = jnp.bfloat16


def positions_of(block_list, block_rows):
    offsets = jnp.arange(block_rows, dtype=jnp.int32)
    return (block_list[:, None] * block_rows + offsets[None, :]).reshape(-1)


def shards(query, key, value, out_weight, out_grad, block_ids):
    tokens_here = query.shape[1]
    width_heads = query.shape[2]
    block_rows = tokens_here // block_ids.shape[0]
    score_scale = 1.0 / math.sqrt(HD)
    all_blocks = lax.all_gather(block_ids, "seq", axis=0, tiled=True)
    query_pos = positions_of(block_ids, block_rows)
    every_pos = positions_of(all_blocks, block_rows)
    key_all, value_all = (
        lax.all_gather(key, "seq", axis=1, tiled=True),
        lax.all_gather(value, "seq", axis=1, tiled=True),
    )
    query_heads = query[0].reshape(tokens_here, HEADS, HD)
    key_heads = key_all[0].reshape(-1, HEADS, HD)
    value_heads = value_all[0].reshape(-1, HEADS, HD)
    scores = (
        jnp.einsum("thd,khd->htk", query_heads, key_heads, preferred_element_type=jnp.float32)
        * score_scale
    )
    allowed = every_pos[None, :] <= query_pos[:, None]
    scores = jnp.where(allowed[None], scores, -jnp.inf)
    row_top = jnp.max(scores, axis=2, keepdims=True)
    row_total = jnp.sum(jnp.exp(scores - row_top), axis=2, keepdims=True)
    log_total = row_top + jnp.log(row_total)
    weights = jnp.exp(scores - log_total)
    weights_low = weights.astype(jnp.bfloat16)
    attended = jnp.einsum(
        "htk,khd->thd", weights_low, value_heads, preferred_element_type=jnp.float32
    ).astype(jnp.bfloat16)
    grad_rows = out_grad[0]
    attn_grad = lax.dot_general(
        grad_rows,
        lax.all_gather(out_weight, "fsdp", axis=0, tiled=True),
        (((1,), (1,)), ((), ())),
        preferred_element_type=jnp.float32,
    ).astype(jnp.bfloat16)
    attended_flat = attended.reshape(tokens_here, width_heads)
    weight_shard = lax.psum_scatter(
        lax.dot_general(
            attended_flat, grad_rows, (((0,), (0,)), ((), ())), preferred_element_type=jnp.float32
        ).astype(jnp.bfloat16),
        "fsdp",
        scatter_dimension=0,
        tiled=True,
    ).astype(jnp.float32)
    token_count = tokens_here * lax.axis_size("seq") * lax.axis_size("fsdp") * lax.axis_size("dp")
    weight_grad = (lax.psum(weight_shard, ("seq", "dp")) * (1.0 / math.sqrt(token_count))).astype(
        jnp.bfloat16
    )
    grad_heads = attn_grad.reshape(tokens_here, HEADS, HD)
    row_delta = jnp.einsum("thd,thd->ht", grad_heads, attended, preferred_element_type=jnp.float32)
    prob_grad = jnp.einsum(
        "thd,khd->htk", grad_heads, value_heads, preferred_element_type=jnp.float32
    )
    score_grad = (weights * (prob_grad - row_delta[:, :, None])).astype(jnp.bfloat16)
    query_grad = (
        jnp.einsum("htk,khd->thd", score_grad, key_heads, preferred_element_type=jnp.float32)
        * score_scale
    ).astype(jnp.bfloat16)
    query_all, grad_all = (
        lax.all_gather(query, "seq", axis=1, tiled=True),
        lax.all_gather(attn_grad[None], "seq", axis=1, tiled=True),
    )
    totals_all, deltas_all = (
        lax.all_gather(log_total[:, :, 0][None], "seq", axis=2, tiled=True),
        lax.all_gather(row_delta[None], "seq", axis=2, tiled=True),
    )
    local_keys = key[0].reshape(tokens_here, HEADS, HD)
    local_values = value[0].reshape(tokens_here, HEADS, HD)
    gathered_queries = query_all[0].reshape(-1, HEADS, HD)
    gathered_grads = grad_all[0].reshape(-1, HEADS, HD)
    back_scores = (
        jnp.einsum("khd,qhd->hkq", local_keys, gathered_queries, preferred_element_type=jnp.float32)
        * score_scale
    )
    back_allowed = query_pos[:, None] <= every_pos[None, :]
    back_scores = jnp.where(back_allowed[None], back_scores, -jnp.inf)
    back_weights = jnp.exp(back_scores - totals_all[0][:, None, :])
    back_low = back_weights.astype(jnp.bfloat16)
    back_prob_grad = jnp.einsum(
        "qhd,khd->hkq", gathered_grads, local_values, preferred_element_type=jnp.float32
    )
    back_score_grad = (back_weights * (back_prob_grad - deltas_all[0][:, None, :])).astype(
        jnp.bfloat16
    )
    key_grad = (
        jnp.einsum(
            "hkq,qhd->khd", back_score_grad, gathered_queries, preferred_element_type=jnp.float32
        )
        * score_scale
    ).astype(jnp.bfloat16)
    value_grad = jnp.einsum(
        "hkq,qhd->khd", back_low, gathered_grads, preferred_element_type=jnp.float32
    ).astype(jnp.bfloat16)
    return (
        query_grad.reshape(tokens_here, width_heads)[None],
        key_grad.reshape(tokens_here, width_heads)[None],
        value_grad.reshape(tokens_here, width_heads)[None],
        weight_grad,
    )


def contract(a, b, da, db):
    return lax.dot_general(a, b, (((da,), (db,)), ((), ())), preferred_element_type=F32)


def fused_kernel(
    sizes, blocks_ref, q_ref, k_ref, v_ref, w_ref, og_ref, dq_ref, dk_ref, dv_ref, dw_ref,
    idg, posc, posr, qg, kg, vg, ogall, ws, dos, dog, prob, atts, attg, dqs, dks, dvs, dka, dva,
    wacc, wpart, wrecv, wfin,
    id_s, id_r, in_s, in_r, og_s, og_r, w_sem, do_s, do_r, at_s, at_r, out_s, out_r,
    ws_s, ws_r, wf_s, wf_r, wx_s, wc_s,
):
    nz, nf, nd, blocks = sizes
    rows = q_ref.shape[0]
    length = rows * nz
    block_rows = length // blocks
    local_heads = HEADS // nz
    cut = HD // nz
    token_count = length * nf * nd
    scale = 1.0 / math.sqrt(HD)
    z, f, d = lax.axis_index("seq"), lax.axis_index("fsdp"), lax.axis_index("dp")
    p = f * nd + d
    plane = nf * nd
    total = nz * plane
    me = z * plane + p
    pending = []

    def at(zz, ff, dd):
        return {"seq": zz, "fsdp": ff, "dp": dd}

    def put(src, dst, ssem, rsem, target, same=None):
        copy = pltpu.make_async_remote_copy(
            src_ref=src, dst_ref=dst, send_sem=ssem, recv_sem=rsem,
            device_id=target, device_id_type=MESH,
        )
        if same is None:
            copy.start()
        else:
            @pl.when(jnp.logical_not(same))
            def _():
                copy.start()

            @pl.when(same)
            def _():
                pltpu.make_async_copy(src, dst, rsem).start()
        pending.append((copy, same))

    def keep(src, dst, sem):
        pltpu.make_async_copy(src, dst, sem).start()

    def arrived(dst, sem):
        pltpu.make_async_copy(dst, dst, sem).wait()

    def band(i):
        return pl.ds(pl.multiple_of(i * rows, rows), rows)

    def head_cols(h):
        return pl.ds(pl.multiple_of(h * HD, HD), HD)

    barrier = pltpu.get_barrier_semaphore()

    def greet(i, c):
        t = lax.rem(me + i, total)
        pl.semaphore_signal(
            barrier, inc=1, device_id=at(t // plane, (t // nd) % nf, t % nd), device_id_type=MESH
        )
        return c

    keep(w_ref.at[pl.ds(pl.multiple_of(d * HD, HD), HD)], ws, w_sem)
    keep(og_ref, ogall.at[p], og_r.at[p, 0])
    lax.fori_loop(1, total, greet, 0)
    pl.semaphore_wait(barrier, total - 1)

    dx = (d + nd // 2) % nd
    dc = d + 1 - 2 * (d % 2)
    fy = 1 - f
    other = lambda i: i + 1 - 2 * (i % 2)
    py, px, pxy = fy * nd + d, f * nd + dx, fy * nd + dx
    half = rows // 2
    halves = (pl.ds(0, half), pl.ds(half, half))
    put(og_ref, ogall.at[p], og_s.at[0], og_r.at[p, 0], at(z, fy, d))
    put(og_ref, ogall.at[p], og_s.at[1], og_r.at[p, 0], at(z, f, dx))
    for o in range(1, nz):
        t = (z + o) % nz
        put(blocks_ref, idg.at[z], id_s.at[o], id_r.at[z], at(t, f, d))
    triples = ((k_ref, kg), (q_ref, qg), (v_ref, vg))
    for j in range(local_heads):
        for n, (src, dst) in enumerate(triples):
            for o in range(nz):
                t = (z + o) % nz
                piece, place = src.at[:, head_cols(t * local_heads + j)], dst.at[j, band(z)]
                if o == 0:
                    keep(piece, place, in_r.at[n, j, z])
                else:
                    put(piece, place, in_s.at[n, j, o], in_r.at[n, j, z], at(t, f, d))
        if j == 0:
            put(og_ref, ogall.at[p], og_s.at[2], og_r.at[p, 0], at(z, f, dc))

    head = f * nd + d
    head_z, head_j = head // local_heads, head % local_heads

    def grad_of(i):
        dos[i] = contract(ogall[i], ws[...], 1, 1).astype(BF16)
        put(
            dos.at[i], dog.at[head_j, band(z)], do_s.at[len(grads)], do_r.at[head_j, z],
            at(head_z, i // nd, i % nd),
            jnp.logical_and(head_z == z, p == i) if len(grads) == 0 else None,
        )
        grads.append(i)

    grads = []
    arrived(ws, w_sem)
    arrived(ogall.at[p], og_r.at[p, 0])
    grad_of(p)

    ids = blocks_ref[...]
    for o in range(1, nz):
        t = (z + o) % nz
        arrived(idg.at[t], id_r.at[t])
        ids = ids + idg[t]
    along = lax.broadcasted_iota(jnp.int32, posr.shape, 1)
    down = lax.broadcasted_iota(jnp.int32, posc.shape, 0)
    row_pos = jnp.zeros(posr.shape, jnp.int32)
    col_pos = jnp.zeros(posc.shape, jnp.int32)
    for b in range(blocks):
        low, shift = b * block_rows, ids[b : b + 1, :1] * block_rows - b * block_rows
        row_pos = jnp.where((along >= low) & (along < low + block_rows), along + shift, row_pos)
        col_pos = jnp.where((down >= low) & (down < low + block_rows), down + shift, col_pos)
    posr[...] = row_pos
    posc[...] = col_pos

    def forward(j):
        for n, (_, dst) in enumerate(triples):
            for o in range(nz):
                arrived(dst.at[j, band(o)], in_r.at[n, j, o])

        def step(b, c):
            r = band(b)
            s = contract(qg[j, r, :], kg[j], 1, 1) * scale
            s = jnp.where(posr[0:1, :] <= posc[r, :][:, :1], s, -jnp.inf)
            e = jnp.exp(s - jnp.max(s, axis=1, keepdims=True))
            w = e * (1.0 / jnp.sum(e, axis=1, keepdims=True))
            prob[j, r, :] = w
            atts[j, r, :] = contract(w.astype(BF16), vg[j], 1, 0).astype(BF16)
            return c

        lax.fori_loop(0, nz, step, 0)
        h = z * local_heads + j
        hf, hd = h // nd, h % nd
        for o in range(nz):
            t = (z + o) % nz
            put(
                atts.at[j, band(t)], attg.at[p], at_s.at[j, o], at_r.at[p], at(t, hf, hd),
                (h == p) if o == 0 else None,
            )

    def backward(j):
        for o in range(nz):
            arrived(dog.at[j, band(o)], do_r.at[j, o])
        dka[...] = jnp.zeros(dka.shape, F32)
        dva[...] = jnp.zeros(dva.shape, F32)

        def step(b, c):
            r = band(b)
            do = dog[j, r, :]
            w = prob[j, r, :]
            delta = jnp.sum(do.astype(F32) * atts[j, r, :].astype(F32), axis=1, keepdims=True)
            ds = (w * (contract(do, vg[j], 1, 1) - delta)).astype(BF16)
            dqs[j, r, :] = (contract(ds, kg[j], 1, 0) * scale).astype(BF16)
            dka[...] += contract(ds, qg[j, r, :], 0, 0)
            dva[...] += contract(w.astype(BF16), do, 0, 0)
            return c

        lax.fori_loop(0, nz, step, 0)
        dks[j] = (dka[...] * scale).astype(BF16)
        dvs[j] = dva[...].astype(BF16)
        h = z * local_heads + j
        for n, (src, dst) in enumerate(((dqs, dq_ref), (dks, dk_ref), (dvs, dv_ref))):
            for o in range(1, nz + 1):
                t = (z + o) % nz
                piece, place = src.at[j, band(t)], dst.at[:, head_cols(h)]
                if o == nz:
                    keep(piece, place, out_r.at[n, h])
                else:
                    put(piece, place, out_s.at[n, j, o], out_r.at[n, h], at(t, f, d))

    forward(0)

    arrived(ogall.at[py], og_r.at[py, 0])
    put(ogall.at[py, halves[0]], ogall.at[py, halves[0]], og_s.at[3], og_r.at[py, 0], at(z, f, dx))
    put(ogall.at[py], ogall.at[py], og_s.at[4], og_r.at[py, 0], at(z, f, dc))
    arrived(ogall.at[px], og_r.at[px, 0])
    put(ogall.at[px, halves[1]], ogall.at[px, halves[1]], og_s.at[5], og_r.at[px, 1], at(z, fy, d))
    put(ogall.at[px], ogall.at[px], og_s.at[6], og_r.at[px, 0], at(z, f, dc))
    grad_of(py)
    grad_of(px)
    arrived(ogall.at[other(p)], og_r.at[other(p), 0])
    grad_of(other(p))
    for i in (other(py), other(px)):
        arrived(ogall.at[i], og_r.at[i, 0])
        grad_of(i)

    forward(1)

    for n in range(2):
        arrived(ogall.at[pxy, halves[n]], og_r.at[pxy, n])
        put(
            ogall.at[pxy, halves[n]], ogall.at[pxy, halves[n]], og_s.at[7 + n], og_r.at[pxy, n],
            at(z, f, dc),
        )
    grad_of(pxy)
    for n in range(2):
        arrived(ogall.at[other(pxy), halves[n]], og_r.at[other(pxy), n])
    grad_of(other(pxy))

    backward(0)

    for i in range(plane):
        arrived(attg.at[i], at_r.at[i])
    wacc[...] = jnp.zeros(wacc.shape, F32)

    def add(i, c):
        wacc[...] += contract(attg[i], ogall[i], 0, 0)
        return c

    lax.fori_loop(0, plane, add, 0)
    wpart[...] = wacc[...].astype(BF16)

    def cut_rows(i):
        return pl.ds(pl.multiple_of(i * cut, cut), cut)

    for o in range(1, nz):
        t = (z + o) % nz
        put(wpart.at[cut_rows(t)], wrecv.at[z], ws_s.at[o], ws_r.at[z], at(t, f, d))

    backward(1)

    share = wacc[cut_rows(z), :]
    for o in range(1, nz):
        t = (z + o) % nz
        arrived(wrecv.at[t], ws_r.at[t])
        share = share + wrecv[t].astype(F32)
    wfin[...] = (share * (1.0 / math.sqrt(token_count))).astype(BF16)

    def final(dd, zz):
        return dw_ref.at[pl.ds(pl.multiple_of(dd * HD + zz * cut, cut), cut)]

    for o in range(1, nz):
        put(wfin, final(d, z), wf_s.at[o], wf_r.at[d, z], at((z + o) % nz, f, d))
    put(wfin, final(d, z), wx_s.at[0], wf_r.at[d, z], at(z, f, dx))
    put(wfin, final(d, z), wc_s.at[0, 0], wf_r.at[d, z], at(z, f, dc))
    keep(wfin, final(d, z), wf_r.at[d, z])
    for o in range(1, nz):
        t = (z + o) % nz
        arrived(final(d, t), wf_r.at[d, t])
        put(final(d, t), final(d, t), wx_s.at[o], wf_r.at[d, t], at(z, f, dx))
        put(final(d, t), final(d, t), wc_s.at[0, o], wf_r.at[d, t], at(z, f, dc))
    for o in range(nz):
        t = (z + o) % nz
        arrived(final(dx, t), wf_r.at[dx, t])
        put(final(dx, t), final(dx, t), wc_s.at[1, o], wf_r.at[dx, t], at(z, f, dc))
    dxc = other(dx)
    arrived(final(d, z), wf_r.at[d, z])
    for dd in (dc, dxc):
        for o in range(nz):
            arrived(final(dd, o), wf_r.at[dd, o])
    for n, dst in enumerate((dq_ref, dk_ref, dv_ref)):
        for h in range(HEADS):
            arrived(dst.at[:, pl.ds(h * HD, HD)], out_r.at[n, h])
    for copy, same in pending:
        if same is None:
            copy.wait_send()
        else:
            @pl.when(jnp.logical_not(same))
            def _(copy=copy):
                copy.wait_send()


def fused(mesh, query, key, value, out_weight, out_grad, block_ids):
    nz, nf, nd = mesh.shape["seq"], mesh.shape["fsdp"], mesh.shape["dp"]
    rows, width = query.shape[1], query.shape[2]
    model = out_grad.shape[2]
    here = block_ids.shape[0]
    blocks = here * nz
    length = rows * nz
    plane = nf * nd
    local_heads = HEADS // nz
    cut = HD // nz
    first = lax.axis_index("seq") * here
    index = jnp.arange(blocks, dtype=jnp.int32)
    spread = sum(jnp.where(index == first + i, block_ids[i], 0) for i in range(here))
    tile = jnp.broadcast_to(spread[:, None], (blocks, 128))
    dma = pltpu.SemaphoreType.DMA
    vm = pltpu.VMEM
    heads_all = (local_heads, length, HD)
    grads = jax.ShapeDtypeStruct((rows, width), BF16)
    anyspec = pl.BlockSpec(memory_space=pl.ANY)
    dq, dk, dv, dw = pl.pallas_call(
        functools.partial(fused_kernel, (nz, nf, nd, blocks)),
        out_shape=(grads, grads, grads, jax.ShapeDtypeStruct(out_weight.shape, BF16)),
        in_specs=[pl.BlockSpec(memory_space=pltpu.VMEM)] + [anyspec] * 5,
        out_specs=(anyspec,) * 4,
        scratch_shapes=[
            vm((nz, blocks, 128), jnp.int32),
            vm((length, 128), jnp.int32),
            vm((8, length), jnp.int32),
            vm(heads_all, BF16), vm(heads_all, BF16), vm(heads_all, BF16),
            vm((plane, rows, model), BF16),
            vm((HD, model), BF16),
            vm((plane, rows, HD), BF16),
            vm(heads_all, BF16),
            vm((local_heads, length, length), F32),
            vm(heads_all, BF16),
            vm((plane, rows, HD), BF16),
            vm(heads_all, BF16), vm(heads_all, BF16), vm(heads_all, BF16),
            vm((length, HD), F32), vm((length, HD), F32),
            vm((HD, model), F32),
            vm((HD, model), BF16),
            vm((nz, cut, model), BF16),
            vm((cut, model), BF16),
            dma((nz,)), dma((nz,)),
            dma((3, local_heads, nz)), dma((3, local_heads, nz)),
            dma((9,)), dma((plane, 2)),
            dma,
            dma((plane,)), dma((local_heads, nz)),
            dma((local_heads, nz)), dma((plane,)),
            dma((3, local_heads, nz)), dma((3, HEADS)),
            dma((nz,)), dma((nz,)),
            dma((nz,)), dma((nd, nz)),
            dma((nz,)), dma((2, nz)),
        ],
        compiler_params=pltpu.CompilerParams(
            collective_id=0, has_side_effects=True, vmem_limit_bytes=48 * 1024 * 1024
        ),
    )(tile, query[0], key[0], value[0], out_weight, out_grad[0])
    return dq[None], dk[None], dv[None], dw


def solution(mesh):
    in_specs = (
        P(("fsdp", "dp"), "seq", None),
        P(("fsdp", "dp"), "seq", None),
        P(("fsdp", "dp"), "seq", None),
        P("fsdp", None),
        P(("fsdp", "dp"), "seq", None),
        P("seq"),
    )
    out_specs = (
        P(("fsdp", "dp"), "seq", None),
        P(("fsdp", "dp"), "seq", None),
        P(("fsdp", "dp"), "seq", None),
        P("fsdp", None),
    )
    part = shards
    if mesh.shape["fsdp"] == 2 and mesh.shape["dp"] == 4 and mesh.shape["seq"] == 4:
        part = functools.partial(fused, mesh)
    return jax.shard_map(part, mesh=mesh, in_specs=in_specs, out_specs=out_specs, check_vma=False)
```

```python
import functools
import math

import jax
import jax.numpy as jnp
from jax import lax
from jax.experimental import pallas as pl
from jax.experimental.pallas import tpu as pltpu
from jax.sharding import PartitionSpec as P

HEADS = 8
HD = 128
MESH = pl.DeviceIdType.MESH
F32 = jnp.float32
BF16 = jnp.bfloat16


def positions_of(block_list, block_rows):
    offsets = jnp.arange(block_rows, dtype=jnp.int32)
    return (block_list[:, None] * block_rows + offsets[None, :]).reshape(-1)


def shards(query, key, value, out_weight, out_grad, block_ids):
    tokens_here = query.shape[1]
    width_heads = query.shape[2]
    block_rows = tokens_here // block_ids.shape[0]
    score_scale = 1.0 / math.sqrt(HD)
    all_blocks = lax.all_gather(block_ids, "seq", axis=0, tiled=True)
    query_pos = positions_of(block_ids, block_rows)
    every_pos = positions_of(all_blocks, block_rows)
    key_all, value_all = (
        lax.all_gather(key, "seq", axis=1, tiled=True),
        lax.all_gather(value, "seq", axis=1, tiled=True),
    )
    query_heads = query[0].reshape(tokens_here, HEADS, HD)
    key_heads = key_all[0].reshape(-1, HEADS, HD)
    value_heads = value_all[0].reshape(-1, HEADS, HD)
    scores = (
        jnp.einsum("thd,khd->htk", query_heads, key_heads, preferred_element_type=jnp.float32)
        * score_scale
    )
    allowed = every_pos[None, :] <= query_pos[:, None]
    scores = jnp.where(allowed[None], scores, -jnp.inf)
    row_top = jnp.max(scores, axis=2, keepdims=True)
    row_total = jnp.sum(jnp.exp(scores - row_top), axis=2, keepdims=True)
    log_total = row_top + jnp.log(row_total)
    weights = jnp.exp(scores - log_total)
    weights_low = weights.astype(jnp.bfloat16)
    attended = jnp.einsum(
        "htk,khd->thd", weights_low, value_heads, preferred_element_type=jnp.float32
    ).astype(jnp.bfloat16)
    grad_rows = out_grad[0]
    attn_grad = lax.dot_general(
        grad_rows,
        lax.all_gather(out_weight, "fsdp", axis=0, tiled=True),
        (((1,), (1,)), ((), ())),
        preferred_element_type=jnp.float32,
    ).astype(jnp.bfloat16)
    attended_flat = attended.reshape(tokens_here, width_heads)
    weight_shard = lax.psum_scatter(
        lax.dot_general(
            attended_flat, grad_rows, (((0,), (0,)), ((), ())), preferred_element_type=jnp.float32
        ).astype(jnp.bfloat16),
        "fsdp",
        scatter_dimension=0,
        tiled=True,
    ).astype(jnp.float32)
    token_count = tokens_here * lax.axis_size("seq") * lax.axis_size("fsdp") * lax.axis_size("dp")
    weight_grad = (lax.psum(weight_shard, ("seq", "dp")) * (1.0 / math.sqrt(token_count))).astype(
        jnp.bfloat16
    )
    grad_heads = attn_grad.reshape(tokens_here, HEADS, HD)
    row_delta = jnp.einsum("thd,thd->ht", grad_heads, attended, preferred_element_type=jnp.float32)
    prob_grad = jnp.einsum(
        "thd,khd->htk", grad_heads, value_heads, preferred_element_type=jnp.float32
    )
    score_grad = (weights * (prob_grad - row_delta[:, :, None])).astype(jnp.bfloat16)
    query_grad = (
        jnp.einsum("htk,khd->thd", score_grad, key_heads, preferred_element_type=jnp.float32)
        * score_scale
    ).astype(jnp.bfloat16)
    query_all, grad_all = (
        lax.all_gather(query, "seq", axis=1, tiled=True),
        lax.all_gather(attn_grad[None], "seq", axis=1, tiled=True),
    )
    totals_all, deltas_all = (
        lax.all_gather(log_total[:, :, 0][None], "seq", axis=2, tiled=True),
        lax.all_gather(row_delta[None], "seq", axis=2, tiled=True),
    )
    local_keys = key[0].reshape(tokens_here, HEADS, HD)
    local_values = value[0].reshape(tokens_here, HEADS, HD)
    gathered_queries = query_all[0].reshape(-1, HEADS, HD)
    gathered_grads = grad_all[0].reshape(-1, HEADS, HD)
    back_scores = (
        jnp.einsum("khd,qhd->hkq", local_keys, gathered_queries, preferred_element_type=jnp.float32)
        * score_scale
    )
    back_allowed = query_pos[:, None] <= every_pos[None, :]
    back_scores = jnp.where(back_allowed[None], back_scores, -jnp.inf)
    back_weights = jnp.exp(back_scores - totals_all[0][:, None, :])
    back_low = back_weights.astype(jnp.bfloat16)
    back_prob_grad = jnp.einsum(
        "qhd,khd->hkq", gathered_grads, local_values, preferred_element_type=jnp.float32
    )
    back_score_grad = (back_weights * (back_prob_grad - deltas_all[0][:, None, :])).astype(
        jnp.bfloat16
    )
    key_grad = (
        jnp.einsum(
            "hkq,qhd->khd", back_score_grad, gathered_queries, preferred_element_type=jnp.float32
        )
        * score_scale
    ).astype(jnp.bfloat16)
    value_grad = jnp.einsum(
        "hkq,qhd->khd", back_low, gathered_grads, preferred_element_type=jnp.float32
    ).astype(jnp.bfloat16)
    return (
        query_grad.reshape(tokens_here, width_heads)[None],
        key_grad.reshape(tokens_here, width_heads)[None],
        value_grad.reshape(tokens_here, width_heads)[None],
        weight_grad,
    )


def contract(a, b, da, db):
    return lax.dot_general(a, b, (((da,), (db,)), ((), ())), preferred_element_type=F32)


def fused_kernel(
    sizes, ids_ref, q_ref, k_ref, v_ref, w_ref, og_ref, dq_ref, dk_ref, dv_ref, dw_ref,
    blocks_ref, idg, posc, posr, qg, kg, vg, ogall, ws, dos, dog, prob, atts, attg, dqs, dks, dvs, dka, dva,
    wacc, wpart, wrecv, wfin,
    id_s, id_r, in_s, in_r, og_s, og_r, w_sem, do_s, do_r, at_s, at_r, out_s, out_r,
    ws_s, ws_r, wf_s, wf_r, wx_s, wc_s,
):
    nz, nf, nd, blocks = sizes
    rows = q_ref.shape[0]
    length = rows * nz
    block_rows = length // blocks
    local_heads = HEADS // nz
    cut = HD // nz
    token_count = length * nf * nd
    scale = 1.0 / math.sqrt(HD)
    z, f, d = lax.axis_index("seq"), lax.axis_index("fsdp"), lax.axis_index("dp")
    p = f * nd + d
    plane = nf * nd
    total = nz * plane
    me = z * plane + p
    pending = []

    def at(zz, ff, dd):
        return {"seq": zz, "fsdp": ff, "dp": dd}

    def put(src, dst, ssem, rsem, target, same=None):
        copy = pltpu.make_async_remote_copy(
            src_ref=src, dst_ref=dst, send_sem=ssem, recv_sem=rsem,
            device_id=target, device_id_type=MESH,
        )
        if same is None:
            copy.start()
        else:
            @pl.when(jnp.logical_not(same))
            def _():
                copy.start()

            @pl.when(same)
            def _():
                pltpu.make_async_copy(src, dst, rsem).start()
        pending.append((copy, same))

    def keep(src, dst, sem):
        pltpu.make_async_copy(src, dst, sem).start()

    def arrived(dst, sem):
        pltpu.make_async_copy(dst, dst, sem).wait()

    def band(i):
        return pl.ds(pl.multiple_of(i * rows, rows), rows)

    def head_cols(h):
        return pl.ds(pl.multiple_of(h * HD, HD), HD)

    barrier = pltpu.get_barrier_semaphore()

    def greet(i, c):
        t = lax.rem(me + i, total)
        pl.semaphore_signal(
            barrier, inc=1, device_id=at(t // plane, (t // nd) % nf, t % nd), device_id_type=MESH
        )
        return c

    here = blocks // nz
    line = lax.broadcasted_iota(jnp.int32, blocks_ref.shape, 0)
    tile = jnp.zeros(blocks_ref.shape, jnp.int32)
    for i in range(here):
        tile = jnp.where(line == z * here + i, ids_ref[i], tile)
    blocks_ref[...] = tile
    keep(w_ref.at[pl.ds(pl.multiple_of(d * HD, HD), HD)], ws, w_sem)
    keep(og_ref, ogall.at[p], og_r.at[p, 0])
    lax.fori_loop(1, total, greet, 0)
    pl.semaphore_wait(barrier, total - 1)

    dx = (d + nd // 2) % nd
    dc = d + 1 - 2 * (d % 2)
    fy = 1 - f
    other = lambda i: i + 1 - 2 * (i % 2)
    py, px, pxy = fy * nd + d, f * nd + dx, fy * nd + dx
    half = rows // 2
    halves = (pl.ds(0, half), pl.ds(half, half))
    put(og_ref, ogall.at[p], og_s.at[0], og_r.at[p, 0], at(z, fy, d))
    put(og_ref, ogall.at[p], og_s.at[1], og_r.at[p, 0], at(z, f, dx))
    for o in range(1, nz):
        t = (z + o) % nz
        put(blocks_ref, idg.at[z], id_s.at[o], id_r.at[z], at(t, f, d))
    triples = ((k_ref, kg), (q_ref, qg), (v_ref, vg))
    for j in range(local_heads):
        for n, (src, dst) in enumerate(triples):
            for o in range(nz):
                t = (z + o) % nz
                piece, place = src.at[:, head_cols(t * local_heads + j)], dst.at[j, band(z)]
                if o == 0:
                    keep(piece, place, in_r.at[n, j, z])
                else:
                    put(piece, place, in_s.at[n, j, o], in_r.at[n, j, z], at(t, f, d))
        if j == 0:
            put(og_ref, ogall.at[p], og_s.at[2], og_r.at[p, 0], at(z, f, dc))

    head = f * nd + d
    head_z, head_j = head // local_heads, head % local_heads

    def grad_of(i):
        dos[i] = contract(ogall[i], ws[...], 1, 1).astype(BF16)
        put(
            dos.at[i], dog.at[head_j, band(z)], do_s.at[len(grads)], do_r.at[head_j, z],
            at(head_z, i // nd, i % nd),
            jnp.logical_and(head_z == z, p == i) if len(grads) == 0 else None,
        )
        grads.append(i)

    grads = []
    arrived(ws, w_sem)
    arrived(ogall.at[p], og_r.at[p, 0])
    grad_of(p)

    ids = blocks_ref[...]
    for o in range(1, nz):
        t = (z + o) % nz
        arrived(idg.at[t], id_r.at[t])
        ids = ids + idg[t]
    along = lax.broadcasted_iota(jnp.int32, posr.shape, 1)
    down = lax.broadcasted_iota(jnp.int32, posc.shape, 0)
    row_pos = jnp.zeros(posr.shape, jnp.int32)
    col_pos = jnp.zeros(posc.shape, jnp.int32)
    for b in range(blocks):
        low, shift = b * block_rows, ids[b : b + 1, :1] * block_rows - b * block_rows
        row_pos = jnp.where((along >= low) & (along < low + block_rows), along + shift, row_pos)
        col_pos = jnp.where((down >= low) & (down < low + block_rows), down + shift, col_pos)
    posr[...] = row_pos
    posc[...] = col_pos

    def forward(j):
        for n, (_, dst) in enumerate(triples):
            for o in range(nz):
                arrived(dst.at[j, band(o)], in_r.at[n, j, o])

        def step(b, c):
            r = band(b)
            s = contract(qg[j, r, :], kg[j], 1, 1) * scale
            s = jnp.where(posr[0:1, :] <= posc[r, :][:, :1], s, -jnp.inf)
            e = jnp.exp(s - jnp.max(s, axis=1, keepdims=True))
            w = e * (1.0 / jnp.sum(e, axis=1, keepdims=True))
            prob[j, r, :] = w
            atts[j, r, :] = contract(w.astype(BF16), vg[j], 1, 0).astype(BF16)

        h = z * local_heads + j

        def give(o):
            t = (z + o) % nz
            return pltpu.make_async_remote_copy(
                src_ref=atts.at[j, band(t)], dst_ref=attg.at[p], send_sem=at_s.at[j, o],
                recv_sem=at_r.at[p], device_id=at(t, h // nd, h % nd), device_id_type=MESH,
            )

        def turn(o, c):
            step((z + o) % nz, c)
            give(o).start()
            return c

        lax.fori_loop(1, nz, turn, 0)
        step(z, 0)
        pending.extend((give(o), None) for o in range(1, nz))
        put(atts.at[j, band(z)], attg.at[p], at_s.at[j, 0], at_r.at[p], at(z, h // nd, h % nd), h == p)

    def backward(j):
        for o in range(nz):
            arrived(dog.at[j, band(o)], do_r.at[j, o])
        dka[...] = jnp.zeros(dka.shape, F32)
        dva[...] = jnp.zeros(dva.shape, F32)

        def step(b, c):
            r = band(b)
            do = dog[j, r, :]
            w = prob[j, r, :]
            delta = jnp.sum(do.astype(F32) * atts[j, r, :].astype(F32), axis=1, keepdims=True)
            ds = (w * (contract(do, vg[j], 1, 1) - delta)).astype(BF16)
            dqs[j, r, :] = (contract(ds, kg[j], 1, 0) * scale).astype(BF16)
            dka[...] += contract(ds, qg[j, r, :], 0, 0)
            dva[...] += contract(w.astype(BF16), do, 0, 0)

        h = z * local_heads + j

        def give(o):
            t = (z + o) % nz
            return pltpu.make_async_remote_copy(
                src_ref=dqs.at[j, band(t)], dst_ref=dq_ref.at[:, head_cols(h)],
                send_sem=out_s.at[0, j, o], recv_sem=out_r.at[0, h], device_id=at(t, f, d),
                device_id_type=MESH,
            )

        def turn(o, c):
            step((z + o) % nz, c)
            give(o).start()
            return c

        lax.fori_loop(1, nz, turn, 0)
        step(z, 0)
        pending.extend((give(o), None) for o in range(1, nz))
        keep(dqs.at[j, band(z)], dq_ref.at[:, head_cols(h)], out_r.at[0, h])
        dks[j] = (dka[...] * scale).astype(BF16)
        dvs[j] = dva[...].astype(BF16)
        for n, (src, dst) in ((1, (dks, dk_ref)), (2, (dvs, dv_ref))):
            for o in range(1, nz + 1):
                t = (z + o) % nz
                piece, place = src.at[j, band(t)], dst.at[:, head_cols(h)]
                if o == nz:
                    keep(piece, place, out_r.at[n, h])
                else:
                    put(piece, place, out_s.at[n, j, o], out_r.at[n, h], at(t, f, d))

    forward(0)

    arrived(ogall.at[py], og_r.at[py, 0])
    put(ogall.at[py, halves[0]], ogall.at[py, halves[0]], og_s.at[3], og_r.at[py, 0], at(z, f, dx))
    put(ogall.at[py], ogall.at[py], og_s.at[4], og_r.at[py, 0], at(z, f, dc))
    arrived(ogall.at[px], og_r.at[px, 0])
    put(ogall.at[px, halves[1]], ogall.at[px, halves[1]], og_s.at[5], og_r.at[px, 1], at(z, fy, d))
    put(ogall.at[px], ogall.at[px], og_s.at[6], og_r.at[px, 0], at(z, f, dc))
    grad_of(py)
    grad_of(px)
    arrived(ogall.at[other(p)], og_r.at[other(p), 0])
    grad_of(other(p))
    for i in (other(py), other(px)):
        arrived(ogall.at[i], og_r.at[i, 0])
        grad_of(i)

    forward(1)

    for n in range(2):
        arrived(ogall.at[pxy, halves[n]], og_r.at[pxy, n])
        put(
            ogall.at[pxy, halves[n]], ogall.at[pxy, halves[n]], og_s.at[7 + n], og_r.at[pxy, n],
            at(z, f, dc),
        )
    grad_of(pxy)
    for n in range(2):
        arrived(ogall.at[other(pxy), halves[n]], og_r.at[other(pxy), n])
    grad_of(other(pxy))

    for i in range(plane):
        arrived(attg.at[i], at_r.at[i])
    wacc[...] = jnp.zeros(wacc.shape, F32)

    def add(i, c):
        wacc[...] += contract(attg[i], ogall[i], 0, 0)
        return c

    lax.fori_loop(0, plane, add, 0)
    wpart[...] = wacc[...].astype(BF16)

    def cut_rows(i):
        return pl.ds(pl.multiple_of(i * cut, cut), cut)

    for o in range(1, nz):
        t = (z + o) % nz
        put(wpart.at[cut_rows(t)], wrecv.at[z], ws_s.at[o], ws_r.at[z], at(t, f, d))

    backward(0)

    share = wacc[cut_rows(z), :]
    for o in range(1, nz):
        t = (z + o) % nz
        arrived(wrecv.at[t], ws_r.at[t])
        share = share + wrecv[t].astype(F32)
    wfin[...] = (share * (1.0 / math.sqrt(token_count))).astype(BF16)

    def final(dd, zz):
        return dw_ref.at[pl.ds(pl.multiple_of(dd * HD + zz * cut, cut), cut)]

    for o in range(1, nz):
        put(wfin, final(d, z), wf_s.at[o], wf_r.at[d, z], at((z + o) % nz, f, d))
    put(wfin, final(d, z), wx_s.at[0], wf_r.at[d, z], at(z, f, dx))
    put(wfin, final(d, z), wc_s.at[0, 0], wf_r.at[d, z], at(z, f, dc))
    keep(wfin, final(d, z), wf_r.at[d, z])

    backward(1)

    for o in range(1, nz):
        t = (z + o) % nz
        arrived(final(d, t), wf_r.at[d, t])
        put(final(d, t), final(d, t), wx_s.at[o], wf_r.at[d, t], at(z, f, dx))
        put(final(d, t), final(d, t), wc_s.at[0, o], wf_r.at[d, t], at(z, f, dc))
    for o in range(nz):
        t = (z + o) % nz
        arrived(final(dx, t), wf_r.at[dx, t])
        put(final(dx, t), final(dx, t), wc_s.at[1, o], wf_r.at[dx, t], at(z, f, dc))
    dxc = other(dx)
    arrived(final(d, z), wf_r.at[d, z])
    for dd in (dc, dxc):
        for o in range(nz):
            arrived(final(dd, o), wf_r.at[dd, o])
    for n, dst in enumerate((dq_ref, dk_ref, dv_ref)):
        for h in range(HEADS):
            arrived(dst.at[:, pl.ds(h * HD, HD)], out_r.at[n, h])
    for copy, same in pending:
        if same is None:
            copy.wait_send()
        else:
            @pl.when(jnp.logical_not(same))
            def _(copy=copy):
                copy.wait_send()


def fused(mesh, query, key, value, out_weight, out_grad, block_ids):
    nz, nf, nd = mesh.shape["seq"], mesh.shape["fsdp"], mesh.shape["dp"]
    rows, width = query.shape[1], query.shape[2]
    model = out_grad.shape[2]
    here = block_ids.shape[0]
    blocks = here * nz
    length = rows * nz
    plane = nf * nd
    local_heads = HEADS // nz
    cut = HD // nz
    dma = pltpu.SemaphoreType.DMA
    vm = pltpu.VMEM
    heads_all = (local_heads, length, HD)
    grads = jax.ShapeDtypeStruct((rows, width), BF16)
    anyspec = pl.BlockSpec(memory_space=pl.ANY)
    dq, dk, dv, dw = pl.pallas_call(
        functools.partial(fused_kernel, (nz, nf, nd, blocks)),
        out_shape=(grads, grads, grads, jax.ShapeDtypeStruct(out_weight.shape, BF16)),
        in_specs=[pl.BlockSpec(memory_space=pltpu.SMEM)] + [anyspec] * 5,
        out_specs=(anyspec,) * 4,
        scratch_shapes=[
            vm((blocks, 128), jnp.int32),
            vm((nz, blocks, 128), jnp.int32),
            vm((length, 128), jnp.int32),
            vm((8, length), jnp.int32),
            vm(heads_all, BF16), vm(heads_all, BF16), vm(heads_all, BF16),
            vm((plane, rows, model), BF16),
            vm((HD, model), BF16),
            vm((plane, rows, HD), BF16),
            vm(heads_all, BF16),
            vm((local_heads, length, length), F32),
            vm(heads_all, BF16),
            vm((plane, rows, HD), BF16),
            vm(heads_all, BF16), vm(heads_all, BF16), vm(heads_all, BF16),
            vm((length, HD), F32), vm((length, HD), F32),
            vm((HD, model), F32),
            vm((HD, model), BF16),
            vm((nz, cut, model), BF16),
            vm((cut, model), BF16),
            dma((nz,)), dma((nz,)),
            dma((3, local_heads, nz)), dma((3, local_heads, nz)),
            dma((9,)), dma((plane, 2)),
            dma,
            dma((plane,)), dma((local_heads, nz)),
            dma((local_heads, nz)), dma((plane,)),
            dma((3, local_heads, nz)), dma((3, HEADS)),
            dma((nz,)), dma((nz,)),
            dma((nz,)), dma((nd, nz)),
            dma((nz,)), dma((2, nz)),
        ],
        compiler_params=pltpu.CompilerParams(
            collective_id=0, has_side_effects=True, vmem_limit_bytes=60 * 1024 * 1024
        ),
    )(block_ids, query[0], key[0], value[0], out_weight, out_grad[0])
    return dq[None], dk[None], dv[None], dw


def solution(mesh):
    in_specs = (
        P(("fsdp", "dp"), "seq", None),
        P(("fsdp", "dp"), "seq", None),
        P(("fsdp", "dp"), "seq", None),
        P("fsdp", None),
        P(("fsdp", "dp"), "seq", None),
        P("seq"),
    )
    out_specs = (
        P(("fsdp", "dp"), "seq", None),
        P(("fsdp", "dp"), "seq", None),
        P(("fsdp", "dp"), "seq", None),
        P("fsdp", None),
    )
    part = shards
    if mesh.shape["fsdp"] == 2 and mesh.shape["dp"] == 4 and mesh.shape["seq"] == 4:
        part = functools.partial(fused, mesh)
    return jax.shard_map(part, mesh=mesh, in_specs=in_specs, out_specs=out_specs, check_vma=False)
```

```python
import functools
import math

import jax
import jax.numpy as jnp
from jax import lax
from jax.experimental import pallas as pl
from jax.experimental.pallas import tpu as pltpu
from jax.sharding import PartitionSpec as P

HEADS = 8
HD = 128
MESH = pl.DeviceIdType.MESH
F32 = jnp.float32
BF16 = jnp.bfloat16


def positions_of(block_list, block_rows):
    offsets = jnp.arange(block_rows, dtype=jnp.int32)
    return (block_list[:, None] * block_rows + offsets[None, :]).reshape(-1)


def shards(query, key, value, out_weight, out_grad, block_ids):
    tokens_here = query.shape[1]
    width_heads = query.shape[2]
    block_rows = tokens_here // block_ids.shape[0]
    score_scale = 1.0 / math.sqrt(HD)
    all_blocks = lax.all_gather(block_ids, "seq", axis=0, tiled=True)
    query_pos = positions_of(block_ids, block_rows)
    every_pos = positions_of(all_blocks, block_rows)
    key_all, value_all = (
        lax.all_gather(key, "seq", axis=1, tiled=True),
        lax.all_gather(value, "seq", axis=1, tiled=True),
    )
    query_heads = query[0].reshape(tokens_here, HEADS, HD)
    key_heads = key_all[0].reshape(-1, HEADS, HD)
    value_heads = value_all[0].reshape(-1, HEADS, HD)
    scores = (
        jnp.einsum("thd,khd->htk", query_heads, key_heads, preferred_element_type=jnp.float32)
        * score_scale
    )
    allowed = every_pos[None, :] <= query_pos[:, None]
    scores = jnp.where(allowed[None], scores, -jnp.inf)
    row_top = jnp.max(scores, axis=2, keepdims=True)
    row_total = jnp.sum(jnp.exp(scores - row_top), axis=2, keepdims=True)
    log_total = row_top + jnp.log(row_total)
    weights = jnp.exp(scores - log_total)
    weights_low = weights.astype(jnp.bfloat16)
    attended = jnp.einsum(
        "htk,khd->thd", weights_low, value_heads, preferred_element_type=jnp.float32
    ).astype(jnp.bfloat16)
    grad_rows = out_grad[0]
    attn_grad = lax.dot_general(
        grad_rows,
        lax.all_gather(out_weight, "fsdp", axis=0, tiled=True),
        (((1,), (1,)), ((), ())),
        preferred_element_type=jnp.float32,
    ).astype(jnp.bfloat16)
    attended_flat = attended.reshape(tokens_here, width_heads)
    weight_shard = lax.psum_scatter(
        lax.dot_general(
            attended_flat, grad_rows, (((0,), (0,)), ((), ())), preferred_element_type=jnp.float32
        ).astype(jnp.bfloat16),
        "fsdp",
        scatter_dimension=0,
        tiled=True,
    ).astype(jnp.float32)
    token_count = tokens_here * lax.axis_size("seq") * lax.axis_size("fsdp") * lax.axis_size("dp")
    weight_grad = (lax.psum(weight_shard, ("seq", "dp")) * (1.0 / math.sqrt(token_count))).astype(
        jnp.bfloat16
    )
    grad_heads = attn_grad.reshape(tokens_here, HEADS, HD)
    row_delta = jnp.einsum("thd,thd->ht", grad_heads, attended, preferred_element_type=jnp.float32)
    prob_grad = jnp.einsum(
        "thd,khd->htk", grad_heads, value_heads, preferred_element_type=jnp.float32
    )
    score_grad = (weights * (prob_grad - row_delta[:, :, None])).astype(jnp.bfloat16)
    query_grad = (
        jnp.einsum("htk,khd->thd", score_grad, key_heads, preferred_element_type=jnp.float32)
        * score_scale
    ).astype(jnp.bfloat16)
    query_all, grad_all = (
        lax.all_gather(query, "seq", axis=1, tiled=True),
        lax.all_gather(attn_grad[None], "seq", axis=1, tiled=True),
    )
    totals_all, deltas_all = (
        lax.all_gather(log_total[:, :, 0][None], "seq", axis=2, tiled=True),
        lax.all_gather(row_delta[None], "seq", axis=2, tiled=True),
    )
    local_keys = key[0].reshape(tokens_here, HEADS, HD)
    local_values = value[0].reshape(tokens_here, HEADS, HD)
    gathered_queries = query_all[0].reshape(-1, HEADS, HD)
    gathered_grads = grad_all[0].reshape(-1, HEADS, HD)
    back_scores = (
        jnp.einsum("khd,qhd->hkq", local_keys, gathered_queries, preferred_element_type=jnp.float32)
        * score_scale
    )
    back_allowed = query_pos[:, None] <= every_pos[None, :]
    back_scores = jnp.where(back_allowed[None], back_scores, -jnp.inf)
    back_weights = jnp.exp(back_scores - totals_all[0][:, None, :])
    back_low = back_weights.astype(jnp.bfloat16)
    back_prob_grad = jnp.einsum(
        "qhd,khd->hkq", gathered_grads, local_values, preferred_element_type=jnp.float32
    )
    back_score_grad = (back_weights * (back_prob_grad - deltas_all[0][:, None, :])).astype(
        jnp.bfloat16
    )
    key_grad = (
        jnp.einsum(
            "hkq,qhd->khd", back_score_grad, gathered_queries, preferred_element_type=jnp.float32
        )
        * score_scale
    ).astype(jnp.bfloat16)
    value_grad = jnp.einsum(
        "hkq,qhd->khd", back_low, gathered_grads, preferred_element_type=jnp.float32
    ).astype(jnp.bfloat16)
    return (
        query_grad.reshape(tokens_here, width_heads)[None],
        key_grad.reshape(tokens_here, width_heads)[None],
        value_grad.reshape(tokens_here, width_heads)[None],
        weight_grad,
    )


def contract(a, b, da, db):
    return lax.dot_general(a, b, (((da,), (db,)), ((), ())), preferred_element_type=F32)


def fused_kernel(
    sizes, ids_ref, q_ref, k_ref, v_ref, w_ref, og_ref, dq_ref, dk_ref, dv_ref, dw_ref,
    blocks_ref, idg, posc, posr, qg, kg, vg, ogall, ws, dos, dog, prob, atts, attg, dqs, dks, dvs, dka, dva,
    wacc, wpart, wrecv, wfin,
    id_s, id_r, in_s, in_r, og_s, og_r, w_sem, do_s, do_r, at_s, at_r, out_s, out_r,
    ws_s, ws_r, wf_s, wf_r, wx_s, wc_s,
):
    nz, nf, nd, blocks = sizes
    rows = q_ref.shape[0]
    length = rows * nz
    block_rows = length // blocks
    local_heads = HEADS // nz
    cut = HD // nz
    token_count = length * nf * nd
    scale = 1.0 / math.sqrt(HD)
    z, f, d = lax.axis_index("seq"), lax.axis_index("fsdp"), lax.axis_index("dp")
    p = f * nd + d
    plane = nf * nd
    total = nz * plane
    me = z * plane + p
    pending = []

    def at(zz, ff, dd):
        return {"seq": zz, "fsdp": ff, "dp": dd}

    def put(src, dst, ssem, rsem, target, same=None):
        copy = pltpu.make_async_remote_copy(
            src_ref=src, dst_ref=dst, send_sem=ssem, recv_sem=rsem,
            device_id=target, device_id_type=MESH,
        )
        if same is None:
            copy.start()
        else:
            @pl.when(jnp.logical_not(same))
            def _():
                copy.start()

            @pl.when(same)
            def _():
                pltpu.make_async_copy(src, dst, rsem).start()
        pending.append((copy, same))

    def put_if(cond, src, dst, ssem, rsem, target):
        copy = pltpu.make_async_remote_copy(
            src_ref=src, dst_ref=dst, send_sem=ssem, recv_sem=rsem,
            device_id=target, device_id_type=MESH,
        )

        @pl.when(cond)
        def _():
            copy.start()

        pending.append((copy, jnp.logical_not(cond)))

    def keep(src, dst, sem):
        pltpu.make_async_copy(src, dst, sem).start()

    def arrived(dst, sem):
        pltpu.make_async_copy(dst, dst, sem).wait()

    def band(i):
        return pl.ds(pl.multiple_of(i * rows, rows), rows)

    def head_cols(h):
        return pl.ds(pl.multiple_of(h * HD, HD), HD)

    barrier = pltpu.get_barrier_semaphore()

    def greet(i, c):
        t = lax.rem(me + i, total)
        pl.semaphore_signal(
            barrier, inc=1, device_id=at(t // plane, (t // nd) % nf, t % nd), device_id_type=MESH
        )
        return c

    here = blocks // nz
    line = lax.broadcasted_iota(jnp.int32, blocks_ref.shape, 0)
    tile = jnp.zeros(blocks_ref.shape, jnp.int32)
    for i in range(here):
        tile = jnp.where(line == z * here + i, ids_ref[i], tile)
    blocks_ref[...] = tile
    keep(w_ref.at[pl.ds(pl.multiple_of(d * HD, HD), HD)], ws, w_sem)
    keep(og_ref, ogall.at[p], og_r.at[p, 0])
    lax.fori_loop(1, total, greet, 0)
    pl.semaphore_wait(barrier, total - 1)

    dx = (d + nd // 2) % nd
    dc = d + 1 - 2 * (d % 2)
    fy = 1 - f
    other = lambda i: i + 1 - 2 * (i % 2)
    py, px, pxy = fy * nd + d, f * nd + dx, fy * nd + dx
    half = rows // 2
    halves = (pl.ds(0, half), pl.ds(half, half))
    put(og_ref, ogall.at[p], og_s.at[0], og_r.at[p, 0], at(z, fy, d))
    put(og_ref, ogall.at[p], og_s.at[1], og_r.at[p, 0], at(z, f, dx))
    for o in range(1, nz):
        t = (z + o) % nz
        put(blocks_ref, idg.at[z], id_s.at[o], id_r.at[z], at(t, f, d))
    triples = ((k_ref, kg), (q_ref, qg), (v_ref, vg))
    for j in range(local_heads):
        for n, (src, dst) in enumerate(triples):
            for o in range(nz):
                t = (z + o) % nz
                piece, place = src.at[:, head_cols(t * local_heads + j)], dst.at[j, band(z)]
                if o == 0:
                    keep(piece, place, in_r.at[n, j, z])
                else:
                    put(piece, place, in_s.at[n, j, o], in_r.at[n, j, z], at(t, f, d))
        if j == 0:
            put(og_ref, ogall.at[p], og_s.at[2], og_r.at[p, 0], at(z, f, dc))

    head = f * nd + d
    head_z, head_j = head // local_heads, head % local_heads

    def grad_of(i):
        dos[i] = contract(ogall[i], ws[...], 1, 1).astype(BF16)
        put(
            dos.at[i], dog.at[head_j, band(z)], do_s.at[len(grads)], do_r.at[head_j, z],
            at(head_z, i // nd, i % nd),
            jnp.logical_and(head_z == z, p == i) if len(grads) == 0 else None,
        )
        grads.append(i)

    grads = []
    arrived(ws, w_sem)
    arrived(ogall.at[p], og_r.at[p, 0])
    grad_of(p)

    ids = blocks_ref[...]
    for o in range(1, nz):
        t = (z + o) % nz
        arrived(idg.at[t], id_r.at[t])
        ids = ids + idg[t]
    along = lax.broadcasted_iota(jnp.int32, posr.shape, 1)
    down = lax.broadcasted_iota(jnp.int32, posc.shape, 0)
    row_pos = jnp.zeros(posr.shape, jnp.int32)
    col_pos = jnp.zeros(posc.shape, jnp.int32)
    for b in range(blocks):
        low, shift = b * block_rows, ids[b : b + 1, :1] * block_rows - b * block_rows
        row_pos = jnp.where((along >= low) & (along < low + block_rows), along + shift, row_pos)
        col_pos = jnp.where((down >= low) & (down < low + block_rows), down + shift, col_pos)
    posr[...] = row_pos
    posc[...] = col_pos

    def forward(j):
        for n, (_, dst) in enumerate(triples):
            for o in range(nz):
                arrived(dst.at[j, band(o)], in_r.at[n, j, o])

        def step(b, c):
            r = band(b)
            s = contract(qg[j, r, :], kg[j], 1, 1) * scale
            s = jnp.where(posr[0:1, :] <= posc[r, :][:, :1], s, -jnp.inf)
            e = jnp.exp(s - jnp.max(s, axis=1, keepdims=True))
            w = e * (1.0 / jnp.sum(e, axis=1, keepdims=True))
            prob[j, r, :] = w
            atts[j, r, :] = contract(w.astype(BF16), vg[j], 1, 0).astype(BF16)

        h = z * local_heads + j

        def give(o):
            t = (z + o) % nz
            return pltpu.make_async_remote_copy(
                src_ref=atts.at[j, band(t)], dst_ref=attg.at[p], send_sem=at_s.at[j, o],
                recv_sem=at_r.at[p], device_id=at(t, h // nd, h % nd), device_id_type=MESH,
            )

        def turn(o, c):
            step((z + o) % nz, c)
            give(o).start()
            return c

        lax.fori_loop(1, nz, turn, 0)
        step(z, 0)
        pending.extend((give(o), None) for o in range(1, nz))
        put(atts.at[j, band(z)], attg.at[p], at_s.at[j, 0], at_r.at[p], at(z, h // nd, h % nd), h == p)

    def backward(j, between):
        for o in range(nz):
            arrived(dog.at[j, band(o)], do_r.at[j, o])
        dka[...] = jnp.zeros(dka.shape, F32)
        dva[...] = jnp.zeros(dva.shape, F32)

        def step(b, c):
            r = band(b)
            do = dog[j, r, :]
            w = prob[j, r, :]
            delta = jnp.sum(do.astype(F32) * atts[j, r, :].astype(F32), axis=1, keepdims=True)
            ds = (w * (contract(do, vg[j], 1, 1) - delta)).astype(BF16)
            dqs[j, r, :] = (contract(ds, kg[j], 1, 0) * scale).astype(BF16)
            dka[...] += contract(ds, qg[j, r, :], 0, 0)
            dva[...] += contract(w.astype(BF16), do, 0, 0)

        h = z * local_heads + j

        def give(o):
            t = (z + o) % nz
            return pltpu.make_async_remote_copy(
                src_ref=dqs.at[j, band(t)], dst_ref=dq_ref.at[:, head_cols(h)],
                send_sem=out_s.at[0, j, o], recv_sem=out_r.at[0, h], device_id=at(t, f, d),
                device_id_type=MESH,
            )

        def turn(o, c):
            step((z + o) % nz, c)
            give(o).start()
            return c

        lax.fori_loop(1, nz, turn, 0)
        step(z, 0)
        pending.extend((give(o), None) for o in range(1, nz))
        keep(dqs.at[j, band(z)], dq_ref.at[:, head_cols(h)], out_r.at[0, h])
        dks[j] = (dka[...] * scale).astype(BF16)
        dvs[j] = dva[...].astype(BF16)
        between()
        for n, (src, dst) in ((1, (dks, dk_ref)), (2, (dvs, dv_ref))):
            for o in range(1, nz + 1):
                t = (z + o) % nz
                piece, place = src.at[j, band(t)], dst.at[:, head_cols(h)]
                if o == nz:
                    keep(piece, place, out_r.at[n, h])
                else:
                    put(piece, place, out_s.at[n, j, o], out_r.at[n, h], at(t, f, d))

    forward(0)

    arrived(ogall.at[py], og_r.at[py, 0])
    put(ogall.at[py, halves[0]], ogall.at[py, halves[0]], og_s.at[3], og_r.at[py, 0], at(z, f, dx))
    put(ogall.at[py], ogall.at[py], og_s.at[4], og_r.at[py, 0], at(z, f, dc))
    arrived(ogall.at[px], og_r.at[px, 0])
    put(ogall.at[px, halves[1]], ogall.at[px, halves[1]], og_s.at[5], og_r.at[px, 1], at(z, fy, d))
    put(ogall.at[px], ogall.at[px], og_s.at[6], og_r.at[px, 0], at(z, f, dc))
    grad_of(py)
    grad_of(px)
    arrived(ogall.at[other(p)], og_r.at[other(p), 0])
    grad_of(other(p))
    for i in (other(py), other(px)):
        arrived(ogall.at[i], og_r.at[i, 0])
        grad_of(i)

    forward(1)

    for n in range(2):
        arrived(ogall.at[pxy, halves[n]], og_r.at[pxy, n])
        put(
            ogall.at[pxy, halves[n]], ogall.at[pxy, halves[n]], og_s.at[7 + n], og_r.at[pxy, n],
            at(z, f, dc),
        )
    grad_of(pxy)
    for n in range(2):
        arrived(ogall.at[other(pxy), halves[n]], og_r.at[other(pxy), n])
    grad_of(other(pxy))

    for i in range(plane):
        arrived(attg.at[i], at_r.at[i])
    wacc[...] = jnp.zeros(wacc.shape, F32)

    def add(i, c):
        wacc[...] += contract(attg[i], ogall[i], 0, 0)
        return c

    lax.fori_loop(0, plane, add, 0)
    wpart[...] = wacc[...].astype(BF16)

    def cut_rows(i):
        return pl.ds(pl.multiple_of(i * cut, cut), cut)

    z1 = z + 1 - 2 * (z % 2)
    z2, z3 = (z + 2) % nz, (z1 + 2) % nz
    put(wpart.at[cut_rows(z3)], wrecv.at[1], ws_s.at[1], ws_r.at[1], at(z1, f, d))
    put(wpart.at[cut_rows(z1)], wrecv.at[0], ws_s.at[0], ws_r.at[0], at(z1, f, d))

    def across():
        arrived(wrecv.at[1], ws_r.at[1])
        wrecv[3] = (wacc[cut_rows(z2), :] + wrecv[1].astype(F32)).astype(BF16)
        put(wrecv.at[3], wrecv.at[2], ws_s.at[2], ws_r.at[2], at(z2, f, d))

    backward(0, across)

    arrived(wrecv.at[0], ws_r.at[0])
    arrived(wrecv.at[2], ws_r.at[2])
    share = wacc[cut_rows(z), :] + wrecv[0].astype(F32) + wrecv[2].astype(F32)
    wfin[...] = (share * (1.0 / math.sqrt(token_count))).astype(BF16)

    def final(dd, zz):
        return dw_ref.at[pl.ds(pl.multiple_of(dd * HD + zz * cut, cut), cut)]

    upper, lower = (z + 1) % nz, (z + nz - 1) % nz
    put_if(z < nz - 1, wfin, final(d, z), wf_s.at[0], wf_r.at[d, z], at(upper, f, d))
    put_if(z > 0, wfin, final(d, z), wf_s.at[1], wf_r.at[d, z], at(lower, f, d))
    put(wfin, final(d, z), wx_s.at[0], wf_r.at[d, z], at(z, f, dx))
    put(wfin, final(d, z), wc_s.at[0, 0], wf_r.at[d, z], at(z, f, dc))
    keep(wfin, final(d, z), wf_r.at[d, z])

    def pass_on(far):
        for side in range(2):
            t = (z - far + nz) % nz if side == 0 else (z + far) % nz
            there = z >= far if side == 0 else z < nz - far
            further = z < nz - 1 if side == 0 else z > 0

            @pl.when(there)
            def _(t=t):
                arrived(final(d, t), wf_r.at[d, t])

            piece, n = final(d, t), 2 * far + side
            put_if(
                jnp.logical_and(there, further), piece, piece, wf_s.at[n], wf_r.at[d, t],
                at(upper if side == 0 else lower, f, d),
            )
            put_if(there, piece, piece, wx_s.at[n], wf_r.at[d, t], at(z, f, dx))
            put_if(there, piece, piece, wc_s.at[0, n], wf_r.at[d, t], at(z, f, dc))

    pass_on(1)
    backward(1, lambda: pass_on(2))
    pass_on(3)
    for o in range(nz):
        t = (z + o) % nz
        arrived(final(dx, t), wf_r.at[dx, t])
        put(final(dx, t), final(dx, t), wc_s.at[1, o], wf_r.at[dx, t], at(z, f, dc))
    dxc = other(dx)
    arrived(final(d, z), wf_r.at[d, z])
    for dd in (dc, dxc):
        for o in range(nz):
            arrived(final(dd, o), wf_r.at[dd, o])
    for n, dst in enumerate((dq_ref, dk_ref, dv_ref)):
        for h in range(HEADS):
            arrived(dst.at[:, pl.ds(h * HD, HD)], out_r.at[n, h])
    for copy, same in pending:
        if same is None:
            copy.wait_send()
        else:
            @pl.when(jnp.logical_not(same))
            def _(copy=copy):
                copy.wait_send()


def hand_out(*refs):
    sources, targets, sems = refs[:4], refs[4:8], refs[8]
    copies = []
    for n in range(4):
        part = sources[n].shape[0] // 4
        for i in range(4):
            rows = pl.ds(i * part, part)
            copies.append(
                pltpu.make_async_copy(sources[n].at[rows], targets[n].at[rows], sems.at[n, i])
            )
    for copy in copies:
        copy.start()
    for copy in copies:
        copy.wait()


def fused(mesh, query, key, value, out_weight, out_grad, block_ids):
    nz, nf, nd = mesh.shape["seq"], mesh.shape["fsdp"], mesh.shape["dp"]
    rows, width = query.shape[1], query.shape[2]
    model = out_grad.shape[2]
    here = block_ids.shape[0]
    blocks = here * nz
    length = rows * nz
    plane = nf * nd
    local_heads = HEADS // nz
    cut = HD // nz
    dma = pltpu.SemaphoreType.DMA
    vm = pltpu.VMEM
    heads_all = (local_heads, length, HD)
    grads = jax.ShapeDtypeStruct((rows, width), BF16)
    anyspec = pl.BlockSpec(memory_space=pl.ANY)
    dq, dk, dv, dw = pl.pallas_call(
        functools.partial(fused_kernel, (nz, nf, nd, blocks)),
        out_shape=(grads, grads, grads, jax.ShapeDtypeStruct(out_weight.shape, BF16)),
        in_specs=[pl.BlockSpec(memory_space=pltpu.SMEM)] + [anyspec] * 5,
        out_specs=(anyspec,) * 4,
        scratch_shapes=[
            vm((blocks, 128), jnp.int32),
            vm((nz, blocks, 128), jnp.int32),
            vm((length, 128), jnp.int32),
            vm((8, length), jnp.int32),
            vm(heads_all, BF16), vm(heads_all, BF16), vm(heads_all, BF16),
            vm((plane, rows, model), BF16),
            vm((HD, model), BF16),
            vm((plane, rows, HD), BF16),
            vm(heads_all, BF16),
            vm((local_heads, length, length), F32),
            vm(heads_all, BF16),
            vm((plane, rows, HD), BF16),
            vm(heads_all, BF16), vm(heads_all, BF16), vm(heads_all, BF16),
            vm((length, HD), F32), vm((length, HD), F32),
            vm((HD, model), F32),
            vm((HD, model), BF16),
            vm((nz, cut, model), BF16),
            vm((cut, model), BF16),
            dma((nz,)), dma((nz,)),
            dma((3, local_heads, nz)), dma((3, local_heads, nz)),
            dma((9,)), dma((plane, 2)),
            dma,
            dma((plane,)), dma((local_heads, nz)),
            dma((local_heads, nz)), dma((plane,)),
            dma((3, local_heads, nz)), dma((3, HEADS)),
            dma((nz,)), dma((nz,)),
            dma((2 * nz,)), dma((nd, nz)),
            dma((2 * nz,)), dma((2, 2 * nz)),
        ],
        compiler_params=pltpu.CompilerParams(
            collective_id=0, has_side_effects=True, vmem_limit_bytes=60 * 1024 * 1024
        ),
    )(block_ids, query[0], key[0], value[0], out_weight, out_grad[0])
    results = (dq, dk, dv, dw)
    dq, dk, dv, dw = pl.pallas_call(
        hand_out,
        out_shape=tuple(jax.ShapeDtypeStruct(r.shape, BF16) for r in results),
        in_specs=[anyspec] * 4,
        out_specs=(anyspec,) * 4,
        scratch_shapes=[dma((4, 4))],
    )(*results)
    return dq[None], dk[None], dv[None], dw


def solution(mesh):
    in_specs = (
        P(("fsdp", "dp"), "seq", None),
        P(("fsdp", "dp"), "seq", None),
        P(("fsdp", "dp"), "seq", None),
        P("fsdp", None),
        P(("fsdp", "dp"), "seq", None),
        P("seq"),
    )
    out_specs = (
        P(("fsdp", "dp"), "seq", None),
        P(("fsdp", "dp"), "seq", None),
        P(("fsdp", "dp"), "seq", None),
        P("fsdp", None),
    )
    part = shards
    if mesh.shape["fsdp"] == 2 and mesh.shape["dp"] == 4 and mesh.shape["seq"] == 4:
        part = functools.partial(fused, mesh)
    return jax.shard_map(part, mesh=mesh, in_specs=in_specs, out_specs=out_specs, check_vma=False)
```

```python
import functools
import math

import jax
import jax.numpy as jnp
from jax import lax
from jax.experimental import pallas as pl
from jax.experimental.pallas import tpu as pltpu
from jax.sharding import PartitionSpec as P

HEADS = 8
HD = 128
MESH = pl.DeviceIdType.MESH
F32 = jnp.float32
BF16 = jnp.bfloat16


def positions_of(block_list, block_rows):
    offsets = jnp.arange(block_rows, dtype=jnp.int32)
    return (block_list[:, None] * block_rows + offsets[None, :]).reshape(-1)


def shards(query, key, value, out_weight, out_grad, block_ids):
    tokens_here = query.shape[1]
    width_heads = query.shape[2]
    block_rows = tokens_here // block_ids.shape[0]
    score_scale = 1.0 / math.sqrt(HD)
    all_blocks = lax.all_gather(block_ids, "seq", axis=0, tiled=True)
    query_pos = positions_of(block_ids, block_rows)
    every_pos = positions_of(all_blocks, block_rows)
    key_all, value_all = (
        lax.all_gather(key, "seq", axis=1, tiled=True),
        lax.all_gather(value, "seq", axis=1, tiled=True),
    )
    query_heads = query[0].reshape(tokens_here, HEADS, HD)
    key_heads = key_all[0].reshape(-1, HEADS, HD)
    value_heads = value_all[0].reshape(-1, HEADS, HD)
    scores = (
        jnp.einsum("thd,khd->htk", query_heads, key_heads, preferred_element_type=jnp.float32)
        * score_scale
    )
    allowed = every_pos[None, :] <= query_pos[:, None]
    scores = jnp.where(allowed[None], scores, -jnp.inf)
    row_top = jnp.max(scores, axis=2, keepdims=True)
    row_total = jnp.sum(jnp.exp(scores - row_top), axis=2, keepdims=True)
    log_total = row_top + jnp.log(row_total)
    weights = jnp.exp(scores - log_total)
    weights_low = weights.astype(jnp.bfloat16)
    attended = jnp.einsum(
        "htk,khd->thd", weights_low, value_heads, preferred_element_type=jnp.float32
    ).astype(jnp.bfloat16)
    grad_rows = out_grad[0]
    attn_grad = lax.dot_general(
        grad_rows,
        lax.all_gather(out_weight, "fsdp", axis=0, tiled=True),
        (((1,), (1,)), ((), ())),
        preferred_element_type=jnp.float32,
    ).astype(jnp.bfloat16)
    attended_flat = attended.reshape(tokens_here, width_heads)
    weight_shard = lax.psum_scatter(
        lax.dot_general(
            attended_flat, grad_rows, (((0,), (0,)), ((), ())), preferred_element_type=jnp.float32
        ).astype(jnp.bfloat16),
        "fsdp",
        scatter_dimension=0,
        tiled=True,
    ).astype(jnp.float32)
    token_count = tokens_here * lax.axis_size("seq") * lax.axis_size("fsdp") * lax.axis_size("dp")
    weight_grad = (lax.psum(weight_shard, ("seq", "dp")) * (1.0 / math.sqrt(token_count))).astype(
        jnp.bfloat16
    )
    grad_heads = attn_grad.reshape(tokens_here, HEADS, HD)
    row_delta = jnp.einsum("thd,thd->ht", grad_heads, attended, preferred_element_type=jnp.float32)
    prob_grad = jnp.einsum(
        "thd,khd->htk", grad_heads, value_heads, preferred_element_type=jnp.float32
    )
    score_grad = (weights * (prob_grad - row_delta[:, :, None])).astype(jnp.bfloat16)
    query_grad = (
        jnp.einsum("htk,khd->thd", score_grad, key_heads, preferred_element_type=jnp.float32)
        * score_scale
    ).astype(jnp.bfloat16)
    query_all, grad_all = (
        lax.all_gather(query, "seq", axis=1, tiled=True),
        lax.all_gather(attn_grad[None], "seq", axis=1, tiled=True),
    )
    totals_all, deltas_all = (
        lax.all_gather(log_total[:, :, 0][None], "seq", axis=2, tiled=True),
        lax.all_gather(row_delta[None], "seq", axis=2, tiled=True),
    )
    local_keys = key[0].reshape(tokens_here, HEADS, HD)
    local_values = value[0].reshape(tokens_here, HEADS, HD)
    gathered_queries = query_all[0].reshape(-1, HEADS, HD)
    gathered_grads = grad_all[0].reshape(-1, HEADS, HD)
    back_scores = (
        jnp.einsum("khd,qhd->hkq", local_keys, gathered_queries, preferred_element_type=jnp.float32)
        * score_scale
    )
    back_allowed = query_pos[:, None] <= every_pos[None, :]
    back_scores = jnp.where(back_allowed[None], back_scores, -jnp.inf)
    back_weights = jnp.exp(back_scores - totals_all[0][:, None, :])
    back_low = back_weights.astype(jnp.bfloat16)
    back_prob_grad = jnp.einsum(
        "qhd,khd->hkq", gathered_grads, local_values, preferred_element_type=jnp.float32
    )
    back_score_grad = (back_weights * (back_prob_grad - deltas_all[0][:, None, :])).astype(
        jnp.bfloat16
    )
    key_grad = (
        jnp.einsum(
            "hkq,qhd->khd", back_score_grad, gathered_queries, preferred_element_type=jnp.float32
        )
        * score_scale
    ).astype(jnp.bfloat16)
    value_grad = jnp.einsum(
        "hkq,qhd->khd", back_low, gathered_grads, preferred_element_type=jnp.float32
    ).astype(jnp.bfloat16)
    return (
        query_grad.reshape(tokens_here, width_heads)[None],
        key_grad.reshape(tokens_here, width_heads)[None],
        value_grad.reshape(tokens_here, width_heads)[None],
        weight_grad,
    )


def contract(a, b, da, db):
    return lax.dot_general(a, b, (((da,), (db,)), ((), ())), preferred_element_type=F32)


def fused_kernel(
    sizes, ids_ref, q_ref, k_ref, v_ref, w_ref, og_ref, dq_ref, dk_ref, dv_ref, dw_ref,
    blocks_ref, idg, posc, posr, qg, kg, vg, ogall, ws, dos, dog, prob, atts, attg, dqs, dks, dvs, dka, dva,
    wacc, wpart, wrecv, wfin, wall,
    id_s, id_r, in_s, in_r, og_s, og_r, w_sem, do_s, do_r, at_s, at_r, out_s, out_r,
    ws_s, ws_r, wf_s, wf_r, wx_s, wc_s, wo_s,
):
    nz, nf, nd, blocks = sizes
    rows = q_ref.shape[0]
    length = rows * nz
    block_rows = length // blocks
    local_heads = HEADS // nz
    cut = HD // nz
    token_count = length * nf * nd
    scale = 1.0 / math.sqrt(HD)
    z, f, d = lax.axis_index("seq"), lax.axis_index("fsdp"), lax.axis_index("dp")
    p = f * nd + d
    plane = nf * nd
    total = nz * plane
    me = z * plane + p
    pending = []

    def at(zz, ff, dd):
        return {"seq": zz, "fsdp": ff, "dp": dd}

    def put(src, dst, ssem, rsem, target, same=None):
        copy = pltpu.make_async_remote_copy(
            src_ref=src, dst_ref=dst, send_sem=ssem, recv_sem=rsem,
            device_id=target, device_id_type=MESH,
        )
        if same is None:
            copy.start()
        else:
            @pl.when(jnp.logical_not(same))
            def _():
                copy.start()

            @pl.when(same)
            def _():
                pltpu.make_async_copy(src, dst, rsem).start()
        pending.append((copy, same))

    def put_if(cond, src, dst, ssem, rsem, target):
        copy = pltpu.make_async_remote_copy(
            src_ref=src, dst_ref=dst, send_sem=ssem, recv_sem=rsem,
            device_id=target, device_id_type=MESH,
        )

        @pl.when(cond)
        def _():
            copy.start()

        pending.append((copy, jnp.logical_not(cond)))

    def keep(src, dst, sem):
        pltpu.make_async_copy(src, dst, sem).start()

    def arrived(dst, sem):
        pltpu.make_async_copy(dst, dst, sem).wait()

    def band(i):
        return pl.ds(pl.multiple_of(i * rows, rows), rows)

    def head_cols(h):
        return pl.ds(pl.multiple_of(h * HD, HD), HD)

    barrier = pltpu.get_barrier_semaphore()

    def greet(i, c):
        t = lax.rem(me + i, total)
        pl.semaphore_signal(
            barrier, inc=1, device_id=at(t // plane, (t // nd) % nf, t % nd), device_id_type=MESH
        )
        return c

    here = blocks // nz
    line = lax.broadcasted_iota(jnp.int32, blocks_ref.shape, 0)
    tile = jnp.zeros(blocks_ref.shape, jnp.int32)
    for i in range(here):
        tile = jnp.where(line == z * here + i, ids_ref[i], tile)
    blocks_ref[...] = tile
    keep(w_ref.at[pl.ds(pl.multiple_of(d * HD, HD), HD)], ws, w_sem)
    keep(og_ref, ogall.at[p], og_r.at[p, 0])
    lax.fori_loop(1, total, greet, 0)
    pl.semaphore_wait(barrier, total - 1)

    dx = (d + nd // 2) % nd
    dc = d + 1 - 2 * (d % 2)
    fy = 1 - f
    other = lambda i: i + 1 - 2 * (i % 2)
    py, px, pxy = fy * nd + d, f * nd + dx, fy * nd + dx
    half = rows // 2
    halves = (pl.ds(0, half), pl.ds(half, half))
    put(og_ref, ogall.at[p], og_s.at[0], og_r.at[p, 0], at(z, fy, d))
    put(og_ref, ogall.at[p], og_s.at[1], og_r.at[p, 0], at(z, f, dx))
    for o in range(1, nz):
        t = (z + o) % nz
        put(blocks_ref, idg.at[z], id_s.at[o], id_r.at[z], at(t, f, d))
    triples = ((k_ref, kg), (q_ref, qg), (v_ref, vg))
    for j in range(local_heads):
        for n, (src, dst) in enumerate(triples):
            for o in range(nz):
                t = (z + o) % nz
                piece, place = src.at[:, head_cols(t * local_heads + j)], dst.at[j, band(z)]
                if o == 0:
                    keep(piece, place, in_r.at[n, j, z])
                else:
                    put(piece, place, in_s.at[n, j, o], in_r.at[n, j, z], at(t, f, d))
        if j == 0:
            put(og_ref, ogall.at[p], og_s.at[2], og_r.at[p, 0], at(z, f, dc))

    head = f * nd + d
    head_z, head_j = head // local_heads, head % local_heads

    def grad_of(i):
        dos[i] = contract(ogall[i], ws[...], 1, 1).astype(BF16)
        put(
            dos.at[i], dog.at[head_j, band(z)], do_s.at[len(grads)], do_r.at[head_j, z],
            at(head_z, i // nd, i % nd),
            jnp.logical_and(head_z == z, p == i) if len(grads) == 0 else None,
        )
        grads.append(i)

    grads = []
    arrived(ws, w_sem)
    arrived(ogall.at[p], og_r.at[p, 0])
    grad_of(p)

    ids = blocks_ref[...]
    for o in range(1, nz):
        t = (z + o) % nz
        arrived(idg.at[t], id_r.at[t])
        ids = ids + idg[t]
    along = lax.broadcasted_iota(jnp.int32, posr.shape, 1)
    down = lax.broadcasted_iota(jnp.int32, posc.shape, 0)
    row_pos = jnp.zeros(posr.shape, jnp.int32)
    col_pos = jnp.zeros(posc.shape, jnp.int32)
    for b in range(blocks):
        low, shift = b * block_rows, ids[b : b + 1, :1] * block_rows - b * block_rows
        row_pos = jnp.where((along >= low) & (along < low + block_rows), along + shift, row_pos)
        col_pos = jnp.where((down >= low) & (down < low + block_rows), down + shift, col_pos)
    posr[...] = row_pos
    posc[...] = col_pos

    def forward(j):
        for n, (_, dst) in enumerate(triples):
            for o in range(nz):
                arrived(dst.at[j, band(o)], in_r.at[n, j, o])

        def step(b, c):
            r = band(b)
            s = contract(qg[j, r, :], kg[j], 1, 1) * scale
            s = jnp.where(posr[0:1, :] <= posc[r, :][:, :1], s, -jnp.inf)
            e = jnp.exp(s - jnp.max(s, axis=1, keepdims=True))
            w = e * (1.0 / jnp.sum(e, axis=1, keepdims=True))
            prob[j, r, :] = w
            atts[j, r, :] = contract(w.astype(BF16), vg[j], 1, 0).astype(BF16)

        h = z * local_heads + j

        def give(o):
            t = (z + o) % nz
            return pltpu.make_async_remote_copy(
                src_ref=atts.at[j, band(t)], dst_ref=attg.at[p], send_sem=at_s.at[j, o],
                recv_sem=at_r.at[p], device_id=at(t, h // nd, h % nd), device_id_type=MESH,
            )

        def turn(o, c):
            step((z + o) % nz, c)
            give(o).start()
            return c

        lax.fori_loop(1, nz, turn, 0)
        step(z, 0)
        pending.extend((give(o), None) for o in range(1, nz))
        put(atts.at[j, band(z)], attg.at[p], at_s.at[j, 0], at_r.at[p], at(z, h // nd, h % nd), h == p)

    def backward(j, between):
        for o in range(nz):
            arrived(dog.at[j, band(o)], do_r.at[j, o])
        dka[...] = jnp.zeros(dka.shape, F32)
        dva[...] = jnp.zeros(dva.shape, F32)

        def step(b, c):
            r = band(b)
            do = dog[j, r, :]
            w = prob[j, r, :]
            delta = jnp.sum(do.astype(F32) * atts[j, r, :].astype(F32), axis=1, keepdims=True)
            ds = (w * (contract(do, vg[j], 1, 1) - delta)).astype(BF16)
            dqs[j, r, :] = (contract(ds, kg[j], 1, 0) * scale).astype(BF16)
            dka[...] += contract(ds, qg[j, r, :], 0, 0)
            dva[...] += contract(w.astype(BF16), do, 0, 0)

        h = z * local_heads + j

        def give(o):
            t = (z + o) % nz
            return pltpu.make_async_remote_copy(
                src_ref=dqs.at[j, band(t)], dst_ref=dq_ref.at[:, head_cols(h)],
                send_sem=out_s.at[0, j, o], recv_sem=out_r.at[0, h], device_id=at(t, f, d),
                device_id_type=MESH,
            )

        def turn(o, c):
            step((z + o) % nz, c)
            give(o).start()
            return c

        lax.fori_loop(1, nz, turn, 0)
        step(z, 0)
        pending.extend((give(o), None) for o in range(1, nz))
        keep(dqs.at[j, band(z)], dq_ref.at[:, head_cols(h)], out_r.at[0, h])
        dks[j] = (dka[...] * scale).astype(BF16)
        dvs[j] = dva[...].astype(BF16)
        between()
        for n, (src, dst) in ((1, (dks, dk_ref)), (2, (dvs, dv_ref))):
            for o in range(1, nz + 1):
                t = (z + o) % nz
                piece, place = src.at[j, band(t)], dst.at[:, head_cols(h)]
                if o == nz:
                    keep(piece, place, out_r.at[n, h])
                else:
                    put(piece, place, out_s.at[n, j, o], out_r.at[n, h], at(t, f, d))

    forward(0)

    arrived(ogall.at[py], og_r.at[py, 0])
    put(ogall.at[py, halves[0]], ogall.at[py, halves[0]], og_s.at[3], og_r.at[py, 0], at(z, f, dx))
    put(ogall.at[py], ogall.at[py], og_s.at[4], og_r.at[py, 0], at(z, f, dc))
    arrived(ogall.at[px], og_r.at[px, 0])
    put(ogall.at[px, halves[1]], ogall.at[px, halves[1]], og_s.at[5], og_r.at[px, 1], at(z, fy, d))
    put(ogall.at[px], ogall.at[px], og_s.at[6], og_r.at[px, 0], at(z, f, dc))
    grad_of(py)
    grad_of(px)
    arrived(ogall.at[other(p)], og_r.at[other(p), 0])
    grad_of(other(p))
    for i in (other(py), other(px)):
        arrived(ogall.at[i], og_r.at[i, 0])
        grad_of(i)

    forward(1)

    for n in range(2):
        arrived(ogall.at[pxy, halves[n]], og_r.at[pxy, n])
        put(
            ogall.at[pxy, halves[n]], ogall.at[pxy, halves[n]], og_s.at[7 + n], og_r.at[pxy, n],
            at(z, f, dc),
        )
    grad_of(pxy)
    for n in range(2):
        arrived(ogall.at[other(pxy), halves[n]], og_r.at[other(pxy), n])
    grad_of(other(pxy))

    for i in range(plane):
        arrived(attg.at[i], at_r.at[i])
    wacc[...] = jnp.zeros(wacc.shape, F32)

    def add(i, c):
        wacc[...] += contract(attg[i], ogall[i], 0, 0)
        return c

    lax.fori_loop(0, plane, add, 0)
    wpart[...] = wacc[...].astype(BF16)

    def cut_rows(i):
        return pl.ds(pl.multiple_of(i * cut, cut), cut)

    z1 = z + 1 - 2 * (z % 2)
    z2, z3 = (z + 2) % nz, (z1 + 2) % nz
    put(wpart.at[cut_rows(z3)], wrecv.at[1], ws_s.at[1], ws_r.at[1], at(z1, f, d))
    put(wpart.at[cut_rows(z1)], wrecv.at[0], ws_s.at[0], ws_r.at[0], at(z1, f, d))

    def across():
        arrived(wrecv.at[1], ws_r.at[1])
        wrecv[3] = (wacc[cut_rows(z2), :] + wrecv[1].astype(F32)).astype(BF16)
        put(wrecv.at[3], wrecv.at[2], ws_s.at[2], ws_r.at[2], at(z2, f, d))

    backward(0, across)

    arrived(wrecv.at[0], ws_r.at[0])
    arrived(wrecv.at[2], ws_r.at[2])
    share = wacc[cut_rows(z), :] + wrecv[0].astype(F32) + wrecv[2].astype(F32)
    wfin[...] = (share * (1.0 / math.sqrt(token_count))).astype(BF16)

    def final(dd, zz):
        return wall.at[pl.ds(pl.multiple_of(dd * HD + zz * cut, cut), cut)]

    upper, lower = (z + 1) % nz, (z + nz - 1) % nz
    put_if(z < nz - 1, wfin, final(d, z), wf_s.at[0], wf_r.at[d, z], at(upper, f, d))
    put_if(z > 0, wfin, final(d, z), wf_s.at[1], wf_r.at[d, z], at(lower, f, d))
    put(wfin, final(d, z), wx_s.at[0], wf_r.at[d, z], at(z, f, dx))
    put(wfin, final(d, z), wc_s.at[0, 0], wf_r.at[d, z], at(z, f, dc))
    keep(wfin, final(d, z), wf_r.at[d, z])

    def pass_on(far):
        for side in range(2):
            t = (z - far + nz) % nz if side == 0 else (z + far) % nz
            there = z >= far if side == 0 else z < nz - far
            further = z < nz - 1 if side == 0 else z > 0

            @pl.when(there)
            def _(t=t):
                arrived(final(d, t), wf_r.at[d, t])

            piece, n = final(d, t), 2 * far + side
            put_if(
                jnp.logical_and(there, further), piece, piece, wf_s.at[n], wf_r.at[d, t],
                at(upper if side == 0 else lower, f, d),
            )
            put_if(there, piece, piece, wx_s.at[n], wf_r.at[d, t], at(z, f, dx))
            put_if(there, piece, piece, wc_s.at[0, n], wf_r.at[d, t], at(z, f, dc))

    pass_on(1)
    backward(1, lambda: pass_on(2))
    pass_on(3)
    def emit(dd):
        block = pl.ds(pl.multiple_of(dd * HD, HD), HD)
        return pltpu.make_async_copy(wall.at[block], dw_ref.at[block], wo_s.at[dd])

    arrived(final(d, z), wf_r.at[d, z])
    emit(d).start()
    for o in range(nz):
        t = (z + o) % nz
        arrived(final(dx, t), wf_r.at[dx, t])
        put(final(dx, t), final(dx, t), wc_s.at[1, o], wf_r.at[dx, t], at(z, f, dc))
    emit(dx).start()
    for dd in (dc, other(dx)):
        for o in range(nz):
            arrived(final(dd, o), wf_r.at[dd, o])
        emit(dd).start()
    for n, dst in enumerate((dq_ref, dk_ref, dv_ref)):
        for h in range(HEADS):
            arrived(dst.at[:, pl.ds(h * HD, HD)], out_r.at[n, h])
    for dd in range(nd):
        emit(dd).wait()
    for copy, same in pending:
        if same is None:
            copy.wait_send()
        else:
            @pl.when(jnp.logical_not(same))
            def _(copy=copy):
                copy.wait_send()


def hand_out(*refs):
    sources, targets, stages, sems = refs[:4], refs[4:8], refs[8:12], refs[12]
    inward, outward = [], []
    for n in range(4):
        part = sources[n].shape[0] // 4
        for i in range(4):
            rows = pl.ds(i * part, part)
            inward.append(
                pltpu.make_async_copy(sources[n].at[rows], stages[n].at[rows], sems.at[0, n, i])
            )
            outward.append(
                pltpu.make_async_copy(stages[n].at[rows], targets[n].at[rows], sems.at[1, n, i])
            )
    for copy in inward:
        copy.start()
    for first, second in zip(inward, outward):
        first.wait()
        second.start()
    for copy in outward:
        copy.wait()


def fused(mesh, query, key, value, out_weight, out_grad, block_ids):
    nz, nf, nd = mesh.shape["seq"], mesh.shape["fsdp"], mesh.shape["dp"]
    rows, width = query.shape[1], query.shape[2]
    model = out_grad.shape[2]
    here = block_ids.shape[0]
    blocks = here * nz
    length = rows * nz
    plane = nf * nd
    local_heads = HEADS // nz
    cut = HD // nz
    dma = pltpu.SemaphoreType.DMA
    vm = pltpu.VMEM
    heads_all = (local_heads, length, HD)
    grads = jax.ShapeDtypeStruct((rows, width), BF16)
    anyspec = pl.BlockSpec(memory_space=pl.ANY)
    dq, dk, dv, dw = pl.pallas_call(
        functools.partial(fused_kernel, (nz, nf, nd, blocks)),
        out_shape=(grads, grads, grads, jax.ShapeDtypeStruct(out_weight.shape, BF16)),
        in_specs=[pl.BlockSpec(memory_space=pltpu.SMEM)] + [anyspec] * 5,
        out_specs=(anyspec,) * 4,
        scratch_shapes=[
            vm((blocks, 128), jnp.int32),
            vm((nz, blocks, 128), jnp.int32),
            vm((length, 128), jnp.int32),
            vm((8, length), jnp.int32),
            vm(heads_all, BF16), vm(heads_all, BF16), vm(heads_all, BF16),
            vm((plane, rows, model), BF16),
            vm((HD, model), BF16),
            vm((plane, rows, HD), BF16),
            vm(heads_all, BF16),
            vm((local_heads, length, length), F32),
            vm(heads_all, BF16),
            vm((plane, rows, HD), BF16),
            vm(heads_all, BF16), vm(heads_all, BF16), vm(heads_all, BF16),
            vm((length, HD), F32), vm((length, HD), F32),
            vm((HD, model), F32),
            vm((HD, model), BF16),
            vm((nz, cut, model), BF16),
            vm((cut, model), BF16),
            vm(out_weight.shape, BF16),
            dma((nz,)), dma((nz,)),
            dma((3, local_heads, nz)), dma((3, local_heads, nz)),
            dma((9,)), dma((plane, 2)),
            dma,
            dma((plane,)), dma((local_heads, nz)),
            dma((local_heads, nz)), dma((plane,)),
            dma((3, local_heads, nz)), dma((3, HEADS)),
            dma((nz,)), dma((nz,)),
            dma((2 * nz,)), dma((nd, nz)),
            dma((2 * nz,)), dma((2, 2 * nz)),
            dma((nd,)),
        ],
        compiler_params=pltpu.CompilerParams(
            collective_id=0, has_side_effects=True, vmem_limit_bytes=60 * 1024 * 1024
        ),
    )(block_ids, query[0], key[0], value[0], out_weight, out_grad[0])
    results = (dq, dk, dv, dw)
    dq, dk, dv, dw = pl.pallas_call(
        hand_out,
        out_shape=tuple(jax.ShapeDtypeStruct(r.shape, BF16) for r in results),
        in_specs=[anyspec] * 4,
        out_specs=(anyspec,) * 4,
        scratch_shapes=[vm(r.shape, BF16) for r in results] + [dma((2, 4, 4))],
    )(*results)
    return dq[None], dk[None], dv[None], dw


def solution(mesh):
    in_specs = (
        P(("fsdp", "dp"), "seq", None),
        P(("fsdp", "dp"), "seq", None),
        P(("fsdp", "dp"), "seq", None),
        P("fsdp", None),
        P(("fsdp", "dp"), "seq", None),
        P("seq"),
    )
    out_specs = (
        P(("fsdp", "dp"), "seq", None),
        P(("fsdp", "dp"), "seq", None),
        P(("fsdp", "dp"), "seq", None),
        P("fsdp", None),
    )
    part = shards
    if mesh.shape["fsdp"] == 2 and mesh.shape["dp"] == 4 and mesh.shape["seq"] == 4:
        part = functools.partial(fused, mesh)
    return jax.shard_map(part, mesh=mesh, in_specs=in_specs, out_specs=out_specs, check_vma=False)
```
